128 devices in a mesh: section: 8 (over z, core), ctx: 16 (over x, y).
Axes of the slice: x: 4, y: 4, z: 4, core: 2. Of those that a mesh axis runs over, the one named last changes fastest.
Arguments:
- embedded: bfloat16 [4096, 2560], P('ctx')
- finished: bfloat16 [8, 4096, 2560], P('section', 'ctx')
- norm_gain: float32 [8, 2560], P('section'), may hold values from 0.5 to 1.5
- q_weight: bfloat16 [8, 2560, 2560], P('section')
- kv_weight: bfloat16 [8, 2560, 1024], P('section')
- out_gain: float32 [8, 2560], P('section'), may hold values from 0.5 to 1.5
- span_order: int32 [16], replicated, may hold values from 0 to 15, each once
Outputs:
- layer_out: bfloat16 [8, 4096, 2560], P('section', 'ctx')
The draws below stay inside these ranges and needn't reach their ends.
Inputs may be any that keep to these rules, and one draw needn't show every extreme that they name: `span_order`: each ctx index holds a different span.
All inputs are finite; a program needn't handle non-finite values. Where the reference program divides by a largest or mean magnitude, that divisor is 1e-20 or more.
Results may differ from the reference program's by a relative error of at most 0.0095.
Values may be sent and summed in bfloat16 or wider, within the bound.
A program may use at most 128 MiB of HBM per device.

```python
import jax
import jax.numpy as jnp
from jax import lax

MODEL_DIM = 2560
QUERY_HEADS = 20
KEY_VALUE_HEADS = 4
HEAD_DIM = 128
QBLOCK = 128
SPAN_ROWS = 256
TOKEN_TOTAL = 4096
N_SECTION = 8
N_CTX = 16


def draw_embedded(key, part):
    key = jax.random.fold_in(key, 11)
    key_noise = jax.random.fold_in(key, 0)
    noise = jnp.clip(jax.random.normal(key_noise, (TOKEN_TOTAL, MODEL_DIM), jnp.float32), -6.0, 6.0)
    return noise.astype(jnp.bfloat16)


def draw_finished(key, part):
    key = jax.random.fold_in(key, 13)
    key_noise = jax.random.fold_in(key, 0)
    noise = jnp.clip(jax.random.normal(key_noise, (N_SECTION, TOKEN_TOTAL, MODEL_DIM), jnp.float32), -6.0, 6.0)
    return noise.astype(jnp.bfloat16)


def draw_q_weight(key, part):
    key = jax.random.fold_in(key, 21)
    local_portion = jax.random.normal(key, (N_SECTION, MODEL_DIM, KEY_VALUE_HEADS, QUERY_HEADS // KEY_VALUE_HEADS, HEAD_DIM), jnp.float32)
    return (local_portion * MODEL_DIM ** (-0.5)).reshape(N_SECTION, MODEL_DIM, QUERY_HEADS * HEAD_DIM).astype(jnp.bfloat16)


def draw_kv_weight(key, part):
    key = jax.random.fold_in(key, 23)
    leading_key, trailing_key = jax.random.split(key, 2)
    value_portion = jax.random.normal(trailing_key, (N_SECTION, MODEL_DIM, KEY_VALUE_HEADS * HEAD_DIM), jnp.float32) * MODEL_DIM ** (-0.5)
    key_portion = jax.random.normal(leading_key, (N_SECTION, MODEL_DIM, KEY_VALUE_HEADS * HEAD_DIM), jnp.float32) * MODEL_DIM ** (-0.5)
    return jnp.concatenate([key_portion, value_portion], axis=-1).astype(jnp.bfloat16)


def setup_inputs(seed: int = 0) -> dict:
    keys = jax.random.split(jax.random.key(seed), 8)
    embedded = draw_embedded(jax.random.fold_in(keys[7], 71), 0)
    finished = draw_finished(jax.random.fold_in(keys[7], 71), 0)
    norm_gain = jnp.clip(1.0 + 0.1 * jax.random.normal(keys[2], (N_SECTION, MODEL_DIM), jnp.float32), 0.5, 1.5)
    q_weight = draw_q_weight(jax.random.fold_in(keys[7], 71), 0)
    kv_weight = draw_kv_weight(jax.random.fold_in(keys[7], 71), 0)
    out_gain = jnp.clip(1.0 + 0.1 * jax.random.normal(keys[5], (N_SECTION, MODEL_DIM), jnp.float32), 0.5, 1.5)
    span_order = jax.random.permutation(keys[6], N_CTX).astype(jnp.int32)
    return {"embedded": embedded, "finished": finished, "norm_gain": norm_gain, "q_weight": q_weight, "kv_weight": kv_weight, "out_gain": out_gain, "span_order": span_order}


EPSILON = 1e-06
MASK_FILLER = -1e+30

def normalize(vector, gain_row):
    return vector * lax.rsqrt(lax.optimization_barrier(jnp.mean(vector * vector, axis=-1, keepdims=True)) + EPSILON) * gain_row

def block_scaled(hidden_rows):
    count_of_rows, model_width = hidden_rows.shape
    grouped = hidden_rows.astype(jnp.float32).reshape(count_of_rows, model_width // QBLOCK, QBLOCK)
    scale_bf = (lax.optimization_barrier(jnp.max(jnp.abs(grouped), axis=-1)) + EPSILON).astype(jnp.bfloat16)
    coded_rows = (grouped / scale_bf.astype(jnp.float32)[..., None]).astype(jnp.bfloat16)
    return (coded_rows, scale_bf)

def reference(embedded, finished, norm_gain, q_weight, kv_weight, out_gain, span_order):
    group_width = QUERY_HEADS // KEY_VALUE_HEADS
    inv_root = HEAD_DIM ** (-0.5)
    token_order = jnp.repeat(span_order, SPAN_ROWS)
    token_row = jnp.arange(TOKEN_TOTAL) % SPAN_ROWS
    query_rows = jnp.arange(SPAN_ROWS)
    layer_outputs = []
    for section_idx in range(N_SECTION):
        if section_idx == 0:
            hidden_in = embedded.astype(jnp.float32)
        else:
            coded_rows, scale_bf = block_scaled(finished[section_idx - 1])
            hidden_in = (coded_rows.astype(jnp.float32) * scale_bf.astype(jnp.float32)[..., None]).reshape(TOKEN_TOTAL, MODEL_DIM)
        normed = normalize(hidden_in, norm_gain[section_idx]).astype(jnp.bfloat16)
        query_matrix = jnp.dot(normed, q_weight[section_idx], preferred_element_type=jnp.float32).astype(jnp.bfloat16)
        key_value_pair = jnp.dot(normed, kv_weight[section_idx], preferred_element_type=jnp.float32).astype(jnp.bfloat16)
        key_portion = key_value_pair[:, :KEY_VALUE_HEADS * HEAD_DIM].reshape(TOKEN_TOTAL, KEY_VALUE_HEADS, HEAD_DIM).astype(jnp.float32)
        value_portion = key_value_pair[:, KEY_VALUE_HEADS * HEAD_DIM:].reshape(TOKEN_TOTAL, KEY_VALUE_HEADS, HEAD_DIM).astype(jnp.float32)

        def one_slice(query_shard):
            first_row = (query_shard * SPAN_ROWS).astype(jnp.int32)
            query_portion = lax.dynamic_slice_in_dim(query_matrix, first_row, SPAN_ROWS, 0)
            query_portion = query_portion.reshape(SPAN_ROWS, KEY_VALUE_HEADS, group_width, HEAD_DIM).astype(jnp.float32)
            own_order = lax.dynamic_slice_in_dim(span_order, query_shard.astype(jnp.int32), 1)[0]
            scores = jnp.einsum('rkgd,skd->kgrs', query_portion, key_portion) * inv_root
            visible = (token_order[None, :] < own_order) | (token_order[None, :] == own_order) & (token_row[None, :] <= query_rows[:, None])
            scores = jnp.where(visible, scores, MASK_FILLER)
            peak_row = lax.optimization_barrier(jnp.max(scores, axis=-1, keepdims=True))
            weights = jnp.where(visible, jnp.exp(scores - peak_row), 0.0)
            totals = lax.optimization_barrier(jnp.sum(weights, axis=-1))
            probs = weights.astype(jnp.bfloat16).astype(jnp.float32)
            mixed_values = jnp.einsum('kgrs,skd->kgrd', probs, value_portion)
            attended = mixed_values / totals[..., None]
            return attended.transpose(2, 0, 1, 3).reshape(SPAN_ROWS, MODEL_DIM)
        attended = lax.map(one_slice, jnp.arange(N_CTX, dtype=jnp.int32)).reshape(TOKEN_TOTAL, MODEL_DIM)
        output_rows = hidden_in + out_gain[section_idx] * normalize(attended, 1.0)
        layer_outputs.append(output_rows.astype(jnp.bfloat16))
    return jnp.stack(layer_outputs)
```

```python
import functools
import math

import jax
import jax.numpy as jnp
from jax import lax
from jax.experimental import pallas as pl
from jax.experimental.pallas import tpu as pltpu
from jax.sharding import PartitionSpec as P

MESH = pl.DeviceIdType.MESH
QUERY_HEADS = 20
KEY_VALUE_HEADS = 4
GROUP = QUERY_HEADS // KEY_VALUE_HEADS
HEAD_DIM = 128
QBLOCK = 128
EPSILON = 1e-06
MASK_FILLER = -1e30
SIDE = 4
ROWS = 256
MODEL = 2560
HEAD_COLS = GROUP * HEAD_DIM
LANES = GROUP * ROWS
CHUNK = 512
N_CHUNK = MODEL // CHUNK
KV_ROWS = 2 * ROWS
SUM_ROWS = 16
SCORE_LIMIT = 48.0
VALUE_LIMIT = 1e15

NT = (((1,), (1,)), ((), ()))
NN = (((1,), (0,)), ((), ()))


def dotf(left, right, dims=NN):
    return lax.dot_general(left, right, dims, preferred_element_type=jnp.float32)


def placement():
    section, ctx = lax.axis_index("section"), lax.axis_index("ctx")
    core = section % 2
    stride_a, stride_b = 1 + 3 * core, 4 - 3 * core
    x, y = ctx // SIDE, ctx % SIDE
    a = x * core + y * (1 - core)
    b = y * core + x * (1 - core)
    return section, ctx, a, b, stride_a, stride_b


def exchange_kernel(
    embedded, finished, gain, q_weight, kv_weight,
    q_all, kv_all, hidden_out,
    raw, hidden, scaled, q_w, kv_w, q_sum, kv_sum, square_sum, q_out, kv_out,
    raw_send, raw_recv, w_sem, local_sem,
    kv_send, kv_recv, row_send, row_recv, q_send, q_recv,
):
    section, ctx, a, b, stride_a, stride_b = placement()

    def at(a_to, b_to):
        return (section, a_to * stride_a + b_to * stride_b)

    def own_chunk(k):
        cols = pl.ds(pl.multiple_of(k * CHUNK, CHUNK), CHUNK)
        return pltpu.make_async_copy(embedded.at[:, cols], raw.at[:, cols], raw_recv.at[k])

    def hand_off(k):
        cols = pl.ds(pl.multiple_of(k * CHUNK, CHUNK), CHUNK)
        return pltpu.make_async_remote_copy(
            finished.at[:, cols], raw.at[:, cols], raw_send.at[k], raw_recv.at[k],
            device_id=((section + 1) % 8, ctx), device_id_type=MESH,
        )

    def weight_copies(k):
        rows = pl.ds(pl.multiple_of(k * CHUNK, CHUNK), CHUNK)
        return (
            pltpu.make_async_copy(kv_weight.at[rows, :], kv_w.at[rows, :], w_sem.at[0, k]),
            pltpu.make_async_copy(q_weight.at[rows, :], q_w.at[rows, :], w_sem.at[1, k]),
        )

    @pl.when(section == 0)
    def _():
        for k in range(N_CHUNK):
            own_chunk(k).start()

    barrier = pltpu.get_barrier_semaphore()
    for d in range(1, SIDE):
        for peer in (at((a + d) % SIDE, b), at(a, (b + d) % SIDE)):
            pl.semaphore_signal(barrier, inc=1, device_id=peer, device_id_type=MESH)

    @pl.when(section > 0)
    def _():
        pl.semaphore_signal(barrier, inc=1, device_id=(section - 1, ctx), device_id_type=MESH)

    @pl.when(section < 7)
    def _():
        pl.semaphore_signal(barrier, inc=1, device_id=(section + 1, ctx), device_id_type=MESH)

    for k in range(N_CHUNK):
        for copy in weight_copies(k):
            copy.start()

    @pl.when(jnp.logical_and(section > 0, section < 7))
    def _():
        pl.semaphore_wait(barrier, 8)

    @pl.when(jnp.logical_or(section == 0, section == 7))
    def _():
        pl.semaphore_wait(barrier, 7)

    @pl.when(section < 7)
    def _():
        for k in range(N_CHUNK):
            hand_off(k).start()

    kv_sum[...] = jnp.zeros_like(kv_sum)
    q_sum[...] = jnp.zeros_like(q_sum)
    square_sum[...] = jnp.zeros_like(square_sum)
    first = section == 0

    def take_chunk(k):
        @pl.when(section == 0)
        def _():
            own_chunk(k).wait()

        @pl.when(section > 0)
        def _():
            hand_off(k).wait_recv()

        squares = jnp.zeros((ROWS, QBLOCK), jnp.float32)
        for j in range(CHUNK // QBLOCK):
            cols = pl.ds(pl.multiple_of(k * CHUNK + j * QBLOCK, QBLOCK), QBLOCK)
            block = raw[:, cols].astype(jnp.float32)
            scale = (jnp.max(jnp.abs(block), axis=1, keepdims=True) + EPSILON).astype(jnp.bfloat16)
            scale = scale.astype(jnp.float32)
            coded = (block / scale).astype(jnp.bfloat16).astype(jnp.float32)
            rows = jnp.where(first, block, coded * scale)
            hidden[:, cols] = rows
            squares += rows * rows
            scaled[:, cols] = (rows * gain[0:1, cols]).astype(jnp.bfloat16)
        square_sum[...] += squares

    def add_kv(k):
        part = pl.ds(pl.multiple_of(k * CHUNK, CHUNK), CHUNK)
        weight_copies(k)[0].wait()
        kv_sum[...] += dotf(scaled[:, part], kv_w[part, :])

    def add_q(k):
        part = pl.ds(pl.multiple_of(k * CHUNK, CHUNK), CHUNK)
        weight_copies(k)[1].wait()
        for h in range(KEY_VALUE_HEADS):
            cols = slice(h * HEAD_COLS, (h + 1) * HEAD_COLS)
            q_sum[:, cols] += dotf(scaled[:, part], q_w[part, cols])

    def early(k, carry):
        take_chunk(k)
        add_kv(k)
        add_q(k)
        return carry

    lax.fori_loop(0, N_CHUNK - 1, early, 0)
    take_chunk(N_CHUNK - 1)
    hidden_copy = pltpu.make_async_copy(hidden, hidden_out, local_sem.at[0])
    hidden_copy.start()
    add_kv(N_CHUNK - 1)

    mean = jnp.sum(square_sum[...], axis=1, keepdims=True) * (1.0 / MODEL)
    inverse = lax.rsqrt(mean + EPSILON)
    for h in range(KEY_VALUE_HEADS):
        keys = kv_sum[:, h * HEAD_DIM:(h + 1) * HEAD_DIM] * inverse
        kv_out[h, 0:ROWS, :] = keys.astype(jnp.bfloat16)
        first_col = (KEY_VALUE_HEADS + h) * HEAD_DIM
        values = kv_sum[:, first_col:first_col + HEAD_DIM] * inverse
        turned = values.T.astype(jnp.bfloat16)
        kv_out[h, ROWS:ROWS + 128, :] = turned[:, 0:128]
        kv_out[h, ROWS + 128:ROWS + 256, :] = turned[:, 128:256]

    def kv_copy(d):
        return pltpu.make_async_remote_copy(
            kv_out.at[(a + d) % SIDE], kv_all.at[b, a], kv_send.at[d - 1], kv_recv.at[d - 1],
            device_id=at((a + d) % SIDE, b), device_id_type=MESH,
        )

    def row_copy(e, p, source):
        return pltpu.make_async_remote_copy(
            source, kv_all.at[b, (a + SIDE - p) % SIDE], row_send.at[e - 1, p], row_recv.at[e - 1, p],
            device_id=at(a, (b + e) % SIDE), device_id_type=MESH,
        )

    for d in (2, 1, 3):
        kv_copy(d).start()
    own_kv = pltpu.make_async_copy(kv_out.at[a], kv_all.at[b, a], local_sem.at[1])
    own_kv.start()
    for e in (2, 1, 3):
        row_copy(e, 0, kv_out.at[a]).start()

    add_q(N_CHUNK - 1)
    q_scale = inverse * (HEAD_DIM ** -0.5 * math.log2(math.e))
    for h in range(KEY_VALUE_HEADS):
        for g in range(GROUP):
            cols = slice((h * GROUP + g) * HEAD_DIM, (h * GROUP + g + 1) * HEAD_DIM)
            q_out[h, g * ROWS:(g + 1) * ROWS, :] = (q_sum[:, cols] * q_scale).astype(jnp.bfloat16)

    def q_copy(d):
        return pltpu.make_async_remote_copy(
            q_out.at[(a + d) % SIDE], q_all.at[SIDE - d], q_send.at[d - 1], q_recv.at[d - 1],
            device_id=at((a + d) % SIDE, b), device_id_type=MESH,
        )

    for d in (2, 1, 3):
        q_copy(d).start()
    own_q = pltpu.make_async_copy(q_out.at[a], q_all.at[0], local_sem.at[2])
    own_q.start()

    for p in (1, 3, 2):
        kv_copy(p).wait_recv()
        for e in (2, 1, 3):
            row_copy(e, p, kv_all.at[b, (a + SIDE - p) % SIDE]).start()

    hidden_copy.wait()
    own_kv.wait()
    own_q.wait()
    for d in range(1, SIDE):
        q_copy(d).wait()
        kv_copy(d).wait_send()
        for p in range(SIDE):
            row_copy(d, p, kv_out.at[a]).wait()

    @pl.when(section < 7)
    def _():
        for k in range(N_CHUNK):
            hand_off(k).wait_send()


def exchange(embedded, finished, gain, q_weight, kv_weight):
    any_spec = pl.BlockSpec(memory_space=pl.ANY)
    vmem = pltpu.VMEM
    dma = pltpu.SemaphoreType.DMA
    return pl.pallas_call(
        exchange_kernel,
        out_shape=(
            jax.ShapeDtypeStruct((SIDE, LANES, HEAD_DIM), jnp.bfloat16),
            jax.ShapeDtypeStruct((SIDE, SIDE, KV_ROWS, HEAD_DIM), jnp.bfloat16),
            jax.ShapeDtypeStruct((ROWS, MODEL), jnp.float32),
        ),
        in_specs=[any_spec, any_spec, pl.BlockSpec(memory_space=vmem), any_spec, any_spec],
        out_specs=(any_spec, any_spec, any_spec),
        scratch_shapes=[
            vmem((ROWS, MODEL), jnp.bfloat16),
            vmem((ROWS, MODEL), jnp.float32),
            vmem((ROWS, MODEL), jnp.bfloat16),
            vmem((MODEL, MODEL), jnp.bfloat16),
            vmem((MODEL, 2 * KEY_VALUE_HEADS * HEAD_DIM), jnp.bfloat16),
            vmem((ROWS, MODEL), jnp.float32),
            vmem((ROWS, 2 * KEY_VALUE_HEADS * HEAD_DIM), jnp.float32),
            vmem((ROWS, QBLOCK), jnp.float32),
            vmem((SIDE, LANES, HEAD_DIM), jnp.bfloat16),
            vmem((SIDE, KV_ROWS, HEAD_DIM), jnp.bfloat16),
            dma((N_CHUNK,)), dma((N_CHUNK,)), dma((2, N_CHUNK)), dma((3,)),
            dma((3,)), dma((3,)), dma((3, SIDE)), dma((3, SIDE)), dma((3,)), dma((3,)),
        ],
        compiler_params=pltpu.CompilerParams(
            collective_id=0, has_side_effects=True, vmem_limit_bytes=48 << 20
        ),
        cost_estimate=pl.CostEstimate(
            flops=2 * ROWS * MODEL * 3584, bytes_accessed=24 << 20, transcendentals=0
        ),
    )(embedded, finished, gain, q_weight, kv_weight)


def attend_kernel(steps, order, q_hbm, kv_hbm, *refs):
    outs = refs[:len(steps)]
    queries, kv, total, peak, slot_of, flag, sems = refs[len(steps):]
    _, _, a, b, stride_a, stride_b = placement()
    kv_copy = pltpu.make_async_copy(kv_hbm, kv, sems.at[0])
    kv_copy.start()
    q_copies = [
        pltpu.make_async_copy(q_hbm.at[e], queries.at[i], sems.at[1 + i]) for i, e in enumerate(steps)
    ]
    for copy in q_copies:
        copy.start()
    for b_of in range(SIDE):
        for a_of in range(SIDE):
            slot_of[order[a_of * stride_a + b_of * stride_b]] = b_of * SIDE + a_of

    kv_copy.wait()
    for copy in q_copies:
        copy.wait()

    ones = jnp.ones((SUM_ROWS, HEAD_DIM), jnp.bfloat16)

    def longest(rows):
        wide = rows.astype(jnp.float32)
        return jnp.max(dotf(ones, (wide * wide).astype(jnp.bfloat16), NT))

    def widest(slot, most):
        values = kv[slot, ROWS:KV_ROWS, :]
        return (
            jnp.maximum(most[0], longest(kv[slot, 0:ROWS, :])),
            jnp.maximum(most[1], jnp.max(jnp.abs(values.astype(jnp.float32)))),
        )

    k_most, v_most = lax.fori_loop(0, SIDE * SIDE, widest, (jnp.float32(0), jnp.float32(0)))
    q_most = lax.fori_loop(
        0, len(steps), lambda i, most: jnp.maximum(most, longest(queries[i])), jnp.float32(0)
    )
    small = jnp.logical_and(
        q_most * k_most <= SCORE_LIMIT * SCORE_LIMIT, v_most <= VALUE_LIMIT
    )

    def key_rows(slots):
        return jnp.concatenate([kv[slot, 0:ROWS, :] for slot in slots], axis=0)

    def value_cols(slots):
        parts = []
        for slot in slots:
            for half in range(2):
                first = ROWS + half * HEAD_DIM
                parts.append(jnp.concatenate([kv[slot, first:first + HEAD_DIM, :], ones], axis=0))
        return jnp.concatenate(parts, axis=1)

    def causal():
        key = lax.broadcasted_iota(jnp.int32, (ROWS, LANES), 0)
        query = lax.broadcasted_iota(jnp.int32, (ROWS, LANES), 1) % ROWS
        return key <= query

    for i, e in enumerate(steps):
        rank = order[((a + e) % SIDE) * stride_a + b * stride_b]

        @pl.when(small)
        def _():
            total[...] = jnp.zeros_like(total)

            def four(c, carry):
                slots = [slot_of[4 * c + j] for j in range(4)]
                weights = jnp.exp2(dotf(key_rows(slots), queries[i], NT)).astype(jnp.bfloat16)
                total[...] += dotf(value_cols(slots), weights)
                return carry

            lax.fori_loop(0, rank // 4, four, 0)
            for rest in range(4):

                @pl.when(rank % 4 == rest)
                def _():
                    slots = [slot_of[rank - rest + j] for j in range(rest + 1)]
                    weights = jnp.exp2(dotf(key_rows(slots), queries[i], NT))
                    last = jnp.where(causal(), weights[rest * ROWS:, :], 0.0)
                    if rest:
                        last = jnp.concatenate([weights[:rest * ROWS, :], last], axis=0)
                    total[...] += dotf(value_cols(slots), last.astype(jnp.bfloat16))

        @pl.when(jnp.logical_not(small))
        def _():
            total[...] = jnp.zeros_like(total)
            peak[...] = jnp.full_like(peak, MASK_FILLER)

            def one(t, carry):
                slots = [slot_of[t]]
                scores = dotf(key_rows(slots), queries[i], NT)
                visible = jnp.logical_or(causal(), t < rank)
                scores = jnp.where(visible, scores, MASK_FILLER)
                before = peak[0:1, :]
                now = jnp.maximum(before, jnp.max(scores, axis=0, keepdims=True))
                weights = jnp.where(visible, jnp.exp2(scores - now), 0.0)
                total[...] = total[...] * jnp.exp2(before - now) + dotf(
                    value_cols(slots), weights.astype(jnp.bfloat16)
                )
                peak[0:1, :] = now
                return carry

            lax.fori_loop(0, rank + 1, one, 0)

        for g in range(GROUP):
            lanes = slice(g * ROWS, (g + 1) * ROWS)
            share = total[0:HEAD_DIM, lanes] / total[HEAD_DIM:HEAD_DIM + 1, lanes]
            outs[i][:, g * HEAD_DIM:(g + 1) * HEAD_DIM] = share.T.astype(jnp.bfloat16)


def attend(order, q_all, kv_all, steps):
    any_spec = pl.BlockSpec(memory_space=pl.ANY)
    vmem = pltpu.VMEM
    out = jax.ShapeDtypeStruct((ROWS, HEAD_COLS), jnp.bfloat16)
    n = len(steps)
    return pl.pallas_call(
        functools.partial(attend_kernel, steps),
        out_shape=(out,) * n,
        in_specs=[pl.BlockSpec(memory_space=pltpu.SMEM), any_spec, any_spec],
        out_specs=(pl.BlockSpec(memory_space=vmem),) * n,
        scratch_shapes=[
            vmem((n, LANES, HEAD_DIM), jnp.bfloat16),
            vmem((SIDE * SIDE, KV_ROWS, HEAD_DIM), jnp.bfloat16),
            vmem((HEAD_DIM + SUM_ROWS, LANES), jnp.float32),
            vmem((8, LANES), jnp.float32),
            pltpu.SMEM((SIDE * SIDE,), jnp.int32),
            pltpu.SMEM((1,), jnp.int32),
            pltpu.SemaphoreType.DMA((1 + n,)),
        ],
        compiler_params=pltpu.CompilerParams(vmem_limit_bytes=48 << 20),
        cost_estimate=pl.CostEstimate(
            flops=n * 4 * LANES * HEAD_DIM * 2304, bytes_accessed=3 << 20, transcendentals=n * LANES * 2304
        ),
    )(order, q_all, kv_all.reshape(SIDE * SIDE, KV_ROWS, HEAD_DIM))


def finish_kernel(p0, p1, p2, p3, hidden, gain, out):
    _, _, a, _, _, _ = placement()
    pieces = [p[...].astype(jnp.float32) for p in (p0, p1, p2, p3)]
    squares = sum(jnp.sum(p * p, axis=1, keepdims=True) for p in pieces)
    inverse = lax.rsqrt(squares * (1.0 / MODEL) + EPSILON)
    for d, piece in enumerate(pieces):
        first = pl.multiple_of(((a + SIDE - d) % SIDE) * HEAD_COLS, HEAD_COLS)
        cols = pl.ds(first, HEAD_COLS)
        rows = hidden[:, cols] + gain[0:1, cols] * (piece * inverse)
        out[:, cols] = rows.astype(jnp.bfloat16)


def finish(pieces, hidden, gain):
    tile = 64
    piece = pl.BlockSpec((tile, HEAD_COLS), lambda i: (i, 0))
    whole = pl.BlockSpec((tile, MODEL), lambda i: (i, 0))
    return pl.pallas_call(
        finish_kernel,
        grid=(ROWS // tile,),
        out_shape=jax.ShapeDtypeStruct((ROWS, MODEL), jnp.bfloat16),
        in_specs=[piece] * 4 + [whole, pl.BlockSpec((1, MODEL), lambda i: (0, 0))],
        out_specs=whole,
    )(*pieces, hidden, gain)


def send_along(x, d):
    pairs = []
    for section in range(8):
        for ctx in range(16):
            if section % 2:
                to = (ctx + d * SIDE) % 16
            else:
                to = ctx // SIDE * SIDE + (ctx + d) % SIDE
            pairs.append((section * 16 + ctx, section * 16 + to))
    return lax.ppermute(x, ("section", "ctx"), pairs)


def per_device(embedded, finished, norm_gain, q_weight, kv_weight, out_gain, span_order):
    q_all, kv_all, hidden = exchange(
        embedded, finished[0], norm_gain, q_weight[0], kv_weight[0]
    )
    far, near, back = attend(span_order, q_all, kv_all, (2, 1, 3))
    far, near, back = send_along(far, 2), send_along(near, 1), send_along(back, 3)
    (own,) = attend(span_order, q_all, kv_all, (0,))
    return finish((own, near, far, back), hidden, out_gain)[None]


def solution(mesh):
    placed = (
        P("ctx", None),
        P("section", "ctx", None),
        P("section", None),
        P("section", None, None),
        P("section", None, None),
        P("section", None),
        P(),
    )
    return jax.shard_map(
        per_device, mesh=mesh, in_specs=placed, out_specs=P("section", "ctx", None), check_vma=False
    )
```

```python
import functools
import math

import jax
import jax.numpy as jnp
from jax import lax
from jax.experimental import pallas as pl
from jax.experimental.pallas import tpu as pltpu
from jax.sharding import PartitionSpec as P

MESH = pl.DeviceIdType.MESH
QUERY_HEADS = 20
KEY_VALUE_HEADS = 4
GROUP = QUERY_HEADS // KEY_VALUE_HEADS
HEAD_DIM = 128
QBLOCK = 128
EPSILON = 1e-06
MASK_FILLER = -1e30
SIDE = 4
ROWS = 256
HALF = ROWS // 2
MODEL = 2560
HEAD_COLS = GROUP * HEAD_DIM
LANES = GROUP * ROWS
CHUNK = 512
N_CHUNK = MODEL // CHUNK
SUM_ROWS = 16
KV_PART = 2 * HALF + SUM_ROWS
Q_PART = GROUP * HALF + SUM_ROWS
ORDER = (2, 1, 3, 0)
RELAYED, DIRECT = (0, 1), (2, 0, 1)
MARGIN = 1.02
Q_SCALE = HEAD_DIM ** -0.5 * math.log2(math.e)
SCORE_LIMIT = 48.0
VALUE_LIMIT = 1e15

NT = (((1,), (1,)), ((), ()))
NN = (((1,), (0,)), ((), ()))


def dotf(left, right, dims=NN):
    return lax.dot_general(left, right, dims, preferred_element_type=jnp.float32)


def placement():
    section, ctx = lax.axis_index("section"), lax.axis_index("ctx")
    core = section % 2
    stride_a, stride_b = 1 + 3 * core, 4 - 3 * core
    x, y = ctx // SIDE, ctx % SIDE
    a = x * core + y * (1 - core)
    b = y * core + x * (1 - core)
    return section, ctx, a, b, stride_a, stride_b


def exchange_kernel(
    embedded, finished, gain, q_weight, kv_weight,
    q_all, kv_all, hidden_out,
    raw, hidden, scaled, q_w, kv_w, q_sum, kv_sum, square_sum, q_out, kv_out,
    raw_send, raw_recv, w_sem, hidden_sem, own_sem,
    kv_send, kv_recv, row_send, row_recv, on_send, on_recv, q_send, q_recv,
):
    section, ctx, a, b, stride_a, stride_b = placement()
    everything = pl.ds(0, 2)

    def at(a_to, b_to):
        return (section, a_to * stride_a + b_to * stride_b)

    def area(i, k):
        return (
            pl.ds(i * HALF, HALF),
            pl.ds(pl.multiple_of(k * CHUNK, CHUNK), CHUNK),
        )

    def own_chunk(i, k):
        return pltpu.make_async_copy(embedded.at[area(i, k)], raw.at[area(i, k)], raw_recv.at[i, k])

    def hand_off(i, k):
        return pltpu.make_async_remote_copy(
            finished.at[area(i, k)], raw.at[area(i, k)], raw_send.at[i, k], raw_recv.at[i, k],
            device_id=((section + 1) % 8, ctx), device_id_type=MESH,
        )

    kv_weight_copy = pltpu.make_async_copy(kv_weight, kv_w, w_sem.at[SIDE])

    def q_weight_copy(d):
        h = (a + d) % SIDE
        cols = pl.ds(pl.multiple_of(h * HEAD_COLS, HEAD_COLS), HEAD_COLS)
        return pltpu.make_async_copy(q_weight.at[:, cols], q_w.at[h], w_sem.at[d])

    @pl.when(section == 0)
    def _():
        for i in range(2):
            for k in range(N_CHUNK):
                own_chunk(i, k).start()

    barrier = pltpu.get_barrier_semaphore()

    @pl.when(section > 0)
    def _():
        pl.semaphore_signal(barrier, inc=1, device_id=(section - 1, ctx), device_id_type=MESH)

    @pl.when(section < 7)
    def _():
        pl.semaphore_signal(barrier, inc=1, device_id=(section + 1, ctx), device_id_type=MESH)

    for d in range(1, SIDE):
        for peer in (at((a + d) % SIDE, b), at(a, (b + d) % SIDE)):
            pl.semaphore_signal(barrier, inc=1, device_id=peer, device_id_type=MESH)

    kv_weight_copy.start()
    for d in ORDER:
        q_weight_copy(d).start()

    @pl.when(jnp.logical_and(section > 0, section < 7))
    def _():
        pl.semaphore_wait(barrier, 8)

    @pl.when(jnp.logical_or(section == 0, section == 7))
    def _():
        pl.semaphore_wait(barrier, 7)

    @pl.when(section < 7)
    def _():
        for i in range(2):
            for k in range(N_CHUNK):
                hand_off(i, k).start()

    first = section == 0

    def take_chunk(i, k):
        @pl.when(section == 0)
        def _():
            own_chunk(i, k).wait()

        @pl.when(section > 0)
        def _():
            hand_off(i, k).wait_recv()

        rows = pl.ds(i * HALF, HALF)
        squares = jnp.zeros((HALF, QBLOCK), jnp.float32)
        for j in range(CHUNK // QBLOCK):
            cols = pl.ds(pl.multiple_of(k * CHUNK + j * QBLOCK, QBLOCK), QBLOCK)
            block = raw[rows, cols].astype(jnp.float32)
            scale = (jnp.max(jnp.abs(block), axis=1, keepdims=True) + EPSILON).astype(jnp.bfloat16)
            scale = scale.astype(jnp.float32)
            coded = (block / scale).astype(jnp.bfloat16).astype(jnp.float32)
            taken = jnp.where(first, block, coded * scale)
            hidden[rows, cols] = taken
            squares += taken * taken
            scaled[rows, cols] = (taken * gain[0:1, cols]).astype(jnp.bfloat16)
        square_sum[rows, :] += squares

    def inverse_rms(rows):
        mean = jnp.sum(square_sum[rows, :], axis=1, keepdims=True) * (1.0 / MODEL)
        return lax.rsqrt(mean + EPSILON)

    def filled(value):
        return jnp.broadcast_to(value * MARGIN, (SUM_ROWS // 2, HEAD_DIM))

    def longest_square(rows):
        return jnp.max(jnp.sum(rows * rows, axis=1, keepdims=True), axis=0, keepdims=True)

    def store_kv(i, sums, inverse):
        for h in range(KEY_VALUE_HEADS):
            keys = sums[:, h * HEAD_DIM:(h + 1) * HEAD_DIM] * inverse
            kv_out[h, i, 0:HALF, :] = keys.astype(jnp.bfloat16)
            first_col = (KEY_VALUE_HEADS + h) * HEAD_DIM
            values = sums[:, first_col:first_col + HEAD_DIM] * inverse
            kv_out[h, i, HALF:2 * HALF, :] = values.T.astype(jnp.bfloat16)
            largest = jnp.max(jnp.max(jnp.abs(values), axis=0, keepdims=True), axis=1, keepdims=True)
            bounds = jnp.concatenate([filled(longest_square(keys)), filled(largest)], axis=0)
            kv_out[h, i, 2 * HALF:, :] = bounds.astype(jnp.bfloat16)

    def store_q(h, i, sums, q_scale):
        most = jnp.zeros((1, 1), jnp.float32)
        for g in range(GROUP):
            queries = sums[:, g * HEAD_DIM:(g + 1) * HEAD_DIM] * q_scale
            q_out[h, i, g * HALF:(g + 1) * HALF, :] = queries.astype(jnp.bfloat16)
            most = jnp.maximum(most, longest_square(queries))
        q_out[h, i, GROUP * HALF:, :] = jnp.concatenate([filled(most)] * 2, axis=0).astype(jnp.bfloat16)

    def kv_copy(part, i, d):
        return pltpu.make_async_remote_copy(
            kv_out.at[(a + d) % SIDE, part], kv_all.at[b, a, part], kv_send.at[i, d - 1], kv_recv.at[i, d - 1],
            device_id=at((a + d) % SIDE, b), device_id_type=MESH,
        )

    def source(p):
        return (a + SIDE - p) % SIDE

    def row_copy(part, i, p, way):
        block = kv_out.at[a, part] if p == 0 else kv_all.at[b, source(p), part]
        return pltpu.make_async_remote_copy(
            block, kv_all.at[b, source(p), part], row_send.at[i, p, way], row_recv.at[i, p, way],
            device_id=at(a, (b + (1, 3, 2)[way]) % SIDE), device_id_type=MESH,
        )

    def on_copy(part, i, p):
        way = p % 2
        block = kv_all.at[(b + (3, 1)[way]) % SIDE, source(p), part]
        return pltpu.make_async_remote_copy(
            block, block, on_send.at[i, p], on_recv.at[i, p],
            device_id=at(a, (b + (1, 3)[way]) % SIDE), device_id_type=MESH,
        )

    def q_copy(part, i, d):
        return pltpu.make_async_remote_copy(
            q_out.at[(a + d) % SIDE, part], q_all.at[SIDE - d, part], q_send.at[i, d - 1], q_recv.at[i, d - 1],
            device_id=at((a + d) % SIDE, b), device_id_type=MESH,
        )

    def own_kv(part, i):
        return pltpu.make_async_copy(kv_out.at[a, part], kv_all.at[b, a, part], own_sem.at[0, i])

    def own_q(part, i):
        return pltpu.make_async_copy(q_out.at[a, part], q_all.at[0, part], own_sem.at[1, i])

    def hidden_copy(i):
        rows = pl.ds(i * HALF, HALF)
        return pltpu.make_async_copy(hidden.at[rows, :], hidden_out.at[rows, :], hidden_sem.at[i])

    def send_kv(part, i, ways):
        for d in (2, 1, 3):
            kv_copy(part, i, d).start()
        for way in ways:
            row_copy(part, i, 0, way).start()
        own_kv(part, i).start()

    def spread(part, i, ways):
        for p in (1, 3, 2):
            kv_copy(part, i, p).wait_recv()
            for way in ways:
                row_copy(part, i, p, way).start()

    def pass_on(part, i):
        for p in (0, 1, 3, 2):
            row_copy(part, i, p, p % 2).wait_recv()
            on_copy(part, i, p).start()

    def settle(part, i, ways):
        own_kv(part, i).wait()
        own_q(part, i).wait()
        for d in range(1, SIDE):
            q_copy(part, i, d).wait()
            kv_copy(part, i, d).wait_send()
        for p in range(SIDE):
            if len(ways) == 3:
                for way in ways:
                    row_copy(part, i, p, way).wait()
            else:
                row_copy(part, i, p, 1 - p % 2).wait_recv()
                for way in ways:
                    row_copy(part, i, p, way).wait_send()
                on_copy(part, i, p).wait()

    square_sum[...] = jnp.zeros_like(square_sum)
    waits = jnp.logical_and(section % 2 == 0, section > 0)

    @pl.when(waits)
    def _():
        def add_kv(i, k):
            part = pl.ds(pl.multiple_of(k * CHUNK, CHUNK), CHUNK)
            kv_sum[...] += dotf(scaled[pl.ds(i * HALF, HALF), part], kv_w[part, :])

        def add_q(i, k):
            part = pl.ds(pl.multiple_of(k * CHUNK, CHUNK), CHUNK)
            for h in range(KEY_VALUE_HEADS):
                q_sum[h] += dotf(scaled[pl.ds(i * HALF, HALF), part], q_w[h, part, :])

        def take_and_add_kv(i, k, carry):
            take_chunk(i, k)
            add_kv(i, k)
            return carry

        def q_only(i, k, carry):
            add_q(i, k)
            return carry

        def chunk(i, k, carry):
            take_chunk(i, k)
            add_kv(i, k)
            add_q(i, k)
            return carry

        kv_weight_copy.wait()
        for i in range(2):
            part, rows = pl.ds(i, 1), pl.ds(i * HALF, HALF)
            kv_sum[...] = jnp.zeros_like(kv_sum)
            q_sum[...] = jnp.zeros_like(q_sum)
            if i == 0:
                lax.fori_loop(0, N_CHUNK, functools.partial(take_and_add_kv, i), 0)
            else:
                lax.fori_loop(0, N_CHUNK - 1, functools.partial(chunk, i), 0)
                take_and_add_kv(i, N_CHUNK - 1, 0)
            inverse = inverse_rms(rows)
            store_kv(i, kv_sum[...], inverse)
            send_kv(part, i, (RELAYED, DIRECT)[i])
            hidden_copy(i).start()
            if i == 0:
                for d in ORDER:
                    q_weight_copy(d).wait()
                lax.fori_loop(0, N_CHUNK, functools.partial(q_only, i), 0)
            else:
                add_q(i, N_CHUNK - 1)
            q_scale = inverse * Q_SCALE
            for d in ORDER:
                h = (a + d) % SIDE
                store_q(h, i, q_sum[h], q_scale)
                if d:
                    q_copy(part, i, d).start()
                else:
                    own_q(part, i).start()
            if i == 0:
                spread(part, i, RELAYED)
        pass_on(pl.ds(0, 1), 0)
        spread(pl.ds(1, 1), 1, DIRECT)
        settle(pl.ds(0, 1), 0, RELAYED)
        settle(pl.ds(1, 1), 1, DIRECT)

    @pl.when(jnp.logical_not(waits))
    def _():
        for i in range(2):
            for k in range(N_CHUNK):
                take_chunk(i, k)
        kv_weight_copy.wait()
        inverse = inverse_rms(pl.ds(0, ROWS))
        sums = dotf(scaled[...], kv_w[...])
        for i in range(2):
            rows = slice(i * HALF, (i + 1) * HALF)
            store_kv(i, sums[rows, :], inverse[rows, :])
        send_kv(everything, 0, RELAYED)
        for i in range(2):
            hidden_copy(i).start()
        q_scale = inverse * Q_SCALE
        for d in ORDER:
            h = (a + d) % SIDE
            q_weight_copy(d).wait()
            group = dotf(scaled[...], q_w[h])
            for i in range(2):
                rows = slice(i * HALF, (i + 1) * HALF)
                store_q(h, i, group[rows, :], q_scale[rows, :])
            if d:
                q_copy(everything, 0, d).start()
            else:
                own_q(everything, 0).start()
        spread(everything, 0, RELAYED)
        pass_on(everything, 0)
        settle(everything, 0, RELAYED)

    for i in range(2):
        hidden_copy(i).wait()

    @pl.when(section < 7)
    def _():
        for i in range(2):
            for k in range(N_CHUNK):
                hand_off(i, k).wait_send()


def exchange(embedded, finished, gain, q_weight, kv_weight):
    hbm = pl.BlockSpec(memory_space=pltpu.HBM)
    vmem = pltpu.VMEM
    dma = pltpu.SemaphoreType.DMA
    return pl.pallas_call(
        exchange_kernel,
        out_shape=(
            jax.ShapeDtypeStruct((SIDE, 2, Q_PART, HEAD_DIM), jnp.bfloat16),
            jax.ShapeDtypeStruct((SIDE, SIDE, 2, KV_PART, HEAD_DIM), jnp.bfloat16),
            jax.ShapeDtypeStruct((ROWS, MODEL), jnp.float32),
        ),
        in_specs=[hbm, hbm, pl.BlockSpec(memory_space=vmem), hbm, hbm],
        out_specs=(hbm, hbm, hbm),
        scratch_shapes=[
            vmem((ROWS, MODEL), jnp.bfloat16),
            vmem((ROWS, MODEL), jnp.float32),
            vmem((ROWS, MODEL), jnp.bfloat16),
            vmem((SIDE, MODEL, HEAD_COLS), jnp.bfloat16),
            vmem((MODEL, 2 * KEY_VALUE_HEADS * HEAD_DIM), jnp.bfloat16),
            vmem((SIDE, HALF, HEAD_COLS), jnp.float32),
            vmem((HALF, 2 * KEY_VALUE_HEADS * HEAD_DIM), jnp.float32),
            vmem((ROWS, QBLOCK), jnp.float32),
            vmem((SIDE, 2, Q_PART, HEAD_DIM), jnp.bfloat16),
            vmem((SIDE, 2, KV_PART, HEAD_DIM), jnp.bfloat16),
            dma((2, N_CHUNK)), dma((2, N_CHUNK)), dma((SIDE + 1,)), dma((2,)), dma((2, 2)),
            dma((2, 3)), dma((2, 3)), dma((2, SIDE, 3)), dma((2, SIDE, 3)),
            dma((2, SIDE)), dma((2, SIDE)), dma((2, 3)), dma((2, 3)),
        ],
        compiler_params=pltpu.CompilerParams(
            collective_id=0, has_side_effects=True, vmem_limit_bytes=60 << 20
        ),
        cost_estimate=pl.CostEstimate(
            flops=2 * ROWS * MODEL * 3584, bytes_accessed=24 << 20, transcendentals=0
        ),
    )(embedded, finished, gain, q_weight, kv_weight)


def attend_kernel(steps, order, q_hbm, kv_hbm, *refs):
    outs = refs[:len(steps)]
    queries, kv, total, peak, slot_of, sems = refs[len(steps):]
    _, _, a, b, stride_a, stride_b = placement()
    kv_copy = pltpu.make_async_copy(kv_hbm, kv, sems.at[0])
    kv_copy.start()
    q_copies = [
        pltpu.make_async_copy(q_hbm.at[e], queries.at[i], sems.at[1 + i]) for i, e in enumerate(steps)
    ]
    for copy in q_copies:
        copy.start()
    for b_of in range(SIDE):
        for a_of in range(SIDE):
            slot_of[order[a_of * stride_a + b_of * stride_b]] = b_of * SIDE + a_of

    kv_copy.wait()
    for copy in q_copies:
        copy.wait()

    ones = jnp.ones((SUM_ROWS, HEAD_DIM), jnp.bfloat16)
    kv_bounds = jnp.max(kv[:, :, 2 * HALF:, :].astype(jnp.float32), axis=(0, 1))
    q_bounds = jnp.max(queries[:, :, GROUP * HALF:, :].astype(jnp.float32), axis=(0, 1))
    small = jnp.logical_and(
        jnp.max(kv_bounds[0:SUM_ROWS // 2, :] * q_bounds[0:SUM_ROWS // 2, :]) <= SCORE_LIMIT * SCORE_LIMIT,
        jnp.max(kv_bounds[SUM_ROWS // 2:, :]) <= VALUE_LIMIT,
    )

    def query_rows(i):
        return jnp.concatenate([queries[i, half, 0:GROUP * HALF, :] for half in range(2)], axis=0)

    def key_rows(slots):
        return jnp.concatenate(
            [kv[slot, half, 0:HALF, :] for slot in slots for half in range(2)], axis=0
        )

    def value_cols(slots):
        parts = [
            jnp.concatenate([kv[slot, half, HALF:2 * HALF, :], ones], axis=0)
            for slot in slots for half in range(2)
        ]
        return jnp.concatenate(parts, axis=1)

    def causal():
        key = lax.broadcasted_iota(jnp.int32, (ROWS, LANES), 0)
        lane = lax.broadcasted_iota(jnp.int32, (ROWS, LANES), 1)
        return key <= lane % HALF + jnp.where(lane >= LANES // 2, HALF, 0)

    def span(i, carry):
        e = steps[0]
        for j in range(1, len(steps)):
            e = jnp.where(i == j, steps[j], e)
        rank = order[((a + e) % SIDE) * stride_a + b * stride_b]

        @pl.when(small)
        def _():
            total[...] = jnp.zeros_like(total)

            def four(c, carry):
                slots = [slot_of[4 * c + j] for j in range(4)]
                weights = jnp.exp2(dotf(key_rows(slots), query_rows(i), NT)).astype(jnp.bfloat16)
                total[...] += dotf(value_cols(slots), weights)
                return carry

            lax.fori_loop(0, rank // 4, four, 0)
            for rest in range(4):

                @pl.when(rank % 4 == rest)
                def _():
                    slots = [slot_of[rank - rest + j] for j in range(rest + 1)]
                    weights = jnp.exp2(dotf(key_rows(slots), query_rows(i), NT))
                    last = jnp.where(causal(), weights[rest * ROWS:, :], 0.0)
                    if rest:
                        last = jnp.concatenate([weights[:rest * ROWS, :], last], axis=0)
                    total[...] += dotf(value_cols(slots), last.astype(jnp.bfloat16))

        @pl.when(jnp.logical_not(small))
        def _():
            total[...] = jnp.zeros_like(total)
            peak[...] = jnp.full_like(peak, MASK_FILLER)

            def one(t, carry):
                slots = [slot_of[t]]
                scores = dotf(key_rows(slots), query_rows(i), NT)
                visible = jnp.logical_or(causal(), t < rank)
                scores = jnp.where(visible, scores, MASK_FILLER)
                before = peak[0:1, :]
                now = jnp.maximum(before, jnp.max(scores, axis=0, keepdims=True))
                weights = jnp.where(visible, jnp.exp2(scores - now), 0.0)
                total[...] = total[...] * jnp.exp2(before - now) + dotf(
                    value_cols(slots), weights.astype(jnp.bfloat16)
                )
                peak[0:1, :] = now
                return carry

            lax.fori_loop(0, rank + 1, one, 0)

        for j in range(len(steps)):

            @pl.when(i == j)
            def _():
                for half in range(2):
                    for g in range(GROUP):
                        first = (half * GROUP + g) * HALF
                        lanes = slice(first, first + HALF)
                        share = total[0:HEAD_DIM, lanes] / total[HEAD_DIM:HEAD_DIM + 1, lanes]
                        rows, cols = slice(half * HALF, (half + 1) * HALF), slice(g * HEAD_DIM, (g + 1) * HEAD_DIM)
                        outs[j][rows, cols] = share.T.astype(jnp.bfloat16)

        return carry

    lax.fori_loop(0, len(steps), span, 0)


def attend(order, q_all, kv_all, steps):
    any_spec = pl.BlockSpec(memory_space=pltpu.HBM)
    vmem = pltpu.VMEM
    out = jax.ShapeDtypeStruct((ROWS, HEAD_COLS), jnp.bfloat16)
    n = len(steps)
    return pl.pallas_call(
        functools.partial(attend_kernel, steps),
        out_shape=(out,) * n,
        in_specs=[pl.BlockSpec(memory_space=pltpu.SMEM), any_spec, any_spec],
        out_specs=(pl.BlockSpec(memory_space=vmem),) * n,
        scratch_shapes=[
            vmem((n, 2, Q_PART, HEAD_DIM), jnp.bfloat16),
            vmem((SIDE * SIDE, 2, KV_PART, HEAD_DIM), jnp.bfloat16),
            vmem((HEAD_DIM + SUM_ROWS, LANES), jnp.float32),
            vmem((8, LANES), jnp.float32),
            pltpu.SMEM((SIDE * SIDE,), jnp.int32),
            pltpu.SemaphoreType.DMA((1 + n,)),
        ],
        compiler_params=pltpu.CompilerParams(vmem_limit_bytes=60 << 20),
        cost_estimate=pl.CostEstimate(
            flops=n * 4 * LANES * HEAD_DIM * 2304, bytes_accessed=3 << 20, transcendentals=n * LANES * 2304
        ),
    )(order, q_all, kv_all.reshape(SIDE * SIDE, 2, KV_PART, HEAD_DIM))


def finish_kernel(p0, p1, p2, p3, hidden, gain, out):
    _, _, a, _, _, _ = placement()
    pieces = [p[...].astype(jnp.float32) for p in (p0, p1, p2, p3)]
    squares = sum(jnp.sum(p * p, axis=1, keepdims=True) for p in pieces)
    inverse = lax.rsqrt(squares * (1.0 / MODEL) + EPSILON)
    for d, piece in enumerate(pieces):
        first = pl.multiple_of(((a + SIDE - d) % SIDE) * HEAD_COLS, HEAD_COLS)
        cols = pl.ds(first, HEAD_COLS)
        rows = hidden[:, cols] + gain[0:1, cols] * (piece * inverse)
        out[:, cols] = rows.astype(jnp.bfloat16)


def finish(pieces, hidden, gain):
    tile = 128
    piece = pl.BlockSpec((tile, HEAD_COLS), lambda i: (i, 0))
    whole = pl.BlockSpec((tile, MODEL), lambda i: (i, 0))
    return pl.pallas_call(
        finish_kernel,
        grid=(ROWS // tile,),
        out_shape=jax.ShapeDtypeStruct((ROWS, MODEL), jnp.bfloat16),
        in_specs=[piece] * 4 + [whole, pl.BlockSpec((1, MODEL), lambda i: (0, 0))],
        out_specs=whole,
        compiler_params=pltpu.CompilerParams(vmem_limit_bytes=60 << 20),
    )(*pieces, hidden, gain)


def send_along(x, d):
    pairs = []
    for section in range(8):
        for ctx in range(16):
            if section % 2:
                to = (ctx + d * SIDE) % 16
            else:
                to = ctx // SIDE * SIDE + (ctx + d) % SIDE
            pairs.append((section * 16 + ctx, section * 16 + to))
    return lax.ppermute(x, ("section", "ctx"), pairs)


def per_device(embedded, finished, norm_gain, q_weight, kv_weight, out_gain, span_order):
    q_all, kv_all, hidden = exchange(
        embedded, finished[0], norm_gain, q_weight[0], kv_weight[0]
    )
    far, near, back = attend(span_order, q_all, kv_all, (2, 1, 3))
    far, near, back = send_along(far, 2), send_along(near, 1), send_along(back, 3)
    (own,) = attend(span_order, q_all, kv_all, (0,))
    return finish((own, near, far, back), hidden, out_gain)[None]


def solution(mesh):
    placed = (
        P("ctx", None),
        P("section", "ctx", None),
        P("section", None),
        P("section", None, None),
        P("section", None, None),
        P("section", None),
        P(),
    )
    return jax.shard_map(
        per_device, mesh=mesh, in_specs=placed, out_specs=P("section", "ctx", None), check_vma=False
    )
```

```python
import functools
import math

import jax
import jax.numpy as jnp
from jax import lax
from jax.experimental import pallas as pl
from jax.experimental.pallas import tpu as pltpu
from jax.sharding import PartitionSpec as P

MESH = pl.DeviceIdType.MESH
QUERY_HEADS = 20
KEY_VALUE_HEADS = 4
GROUP = QUERY_HEADS // KEY_VALUE_HEADS
HEAD_DIM = 128
QBLOCK = 128
EPSILON = 1e-06
MASK_FILLER = -1e30
SIDE = 4
ROWS = 256
HALF = ROWS // 2
MODEL = 2560
HEAD_COLS = GROUP * HEAD_DIM
LANES = GROUP * ROWS
CHUNK = 512
N_CHUNK = MODEL // CHUNK
SUM_ROWS = 16
KV_PART = 2 * HALF + SUM_ROWS
Q_PART = GROUP * HALF + SUM_ROWS
ORDER = (2, 1, 3, 0)
RELAYED, DIRECT = (0, 1), (2, 0, 1)
MARGIN = 1.02
Q_SCALE = HEAD_DIM ** -0.5 * math.log2(math.e)
SCORE_LIMIT = 48.0
VALUE_LIMIT = 1e15

NT = (((1,), (1,)), ((), ()))
NN = (((1,), (0,)), ((), ()))


def dotf(left, right, dims=NN):
    return lax.dot_general(left, right, dims, preferred_element_type=jnp.float32)


def placement():
    section, ctx = lax.axis_index("section"), lax.axis_index("ctx")
    core = section % 2
    stride_a, stride_b = 1 + 3 * core, 4 - 3 * core
    x, y = ctx // SIDE, ctx % SIDE
    a = x * core + y * (1 - core)
    b = y * core + x * (1 - core)
    return section, ctx, a, b, stride_a, stride_b


def exchange_kernel(
    embedded, finished, gain, q_weight, kv_weight,
    q_all, kv_all, hidden_out,
    raw, hidden, scaled, q_w, kv_w, q_sum, kv_sum, square_sum, q_out, kv_out,
    raw_send, raw_recv, w_sem, hidden_sem, own_sem,
    kv_send, kv_recv, row_send, row_recv, on_send, on_recv, q_send, q_recv,
):
    section, ctx, a, b, stride_a, stride_b = placement()
    everything = pl.ds(0, 2)

    def at(a_to, b_to):
        return (section, a_to * stride_a + b_to * stride_b)

    def area(i, k):
        return (
            pl.ds(i * HALF, HALF),
            pl.ds(pl.multiple_of(k * CHUNK, CHUNK), CHUNK),
        )

    def own_chunk(i, k):
        return pltpu.make_async_copy(embedded.at[area(i, k)], raw.at[area(i, k)], raw_recv.at[i, k])

    def hand_off(i, k):
        return pltpu.make_async_remote_copy(
            finished.at[area(i, k)], raw.at[area(i, k)], raw_send.at[i, k], raw_recv.at[i, k],
            device_id=((section + 1) % 8, ctx), device_id_type=MESH,
        )

    kv_weight_copy = pltpu.make_async_copy(kv_weight, kv_w, w_sem.at[SIDE])

    def q_weight_copy(d):
        h = (a + d) % SIDE
        cols = pl.ds(pl.multiple_of(h * HEAD_COLS, HEAD_COLS), HEAD_COLS)
        return pltpu.make_async_copy(q_weight.at[:, cols], q_w.at[h], w_sem.at[d])

    @pl.when(section == 0)
    def _():
        for i in range(2):
            for k in range(N_CHUNK):
                own_chunk(i, k).start()

    barrier = pltpu.get_barrier_semaphore()

    @pl.when(section > 0)
    def _():
        pl.semaphore_signal(barrier, inc=1, device_id=(section - 1, ctx), device_id_type=MESH)

    @pl.when(section < 7)
    def _():
        pl.semaphore_signal(barrier, inc=1, device_id=(section + 1, ctx), device_id_type=MESH)

    for d in range(1, SIDE):
        for peer in (at((a + d) % SIDE, b), at(a, (b + d) % SIDE)):
            pl.semaphore_signal(barrier, inc=1, device_id=peer, device_id_type=MESH)

    kv_weight_copy.start()
    for d in ORDER:
        q_weight_copy(d).start()

    @pl.when(jnp.logical_and(section > 0, section < 7))
    def _():
        pl.semaphore_wait(barrier, 8)

    @pl.when(jnp.logical_or(section == 0, section == 7))
    def _():
        pl.semaphore_wait(barrier, 7)

    @pl.when(section < 7)
    def _():
        for i in range(2):
            for k in range(N_CHUNK):
                hand_off(i, k).start()

    first = section == 0

    def take_chunk(i, k):
        @pl.when(section == 0)
        def _():
            own_chunk(i, k).wait()

        @pl.when(section > 0)
        def _():
            hand_off(i, k).wait_recv()

        rows = pl.ds(i * HALF, HALF)
        squares = jnp.zeros((HALF, QBLOCK), jnp.float32)
        for j in range(CHUNK // QBLOCK):
            cols = pl.ds(pl.multiple_of(k * CHUNK + j * QBLOCK, QBLOCK), QBLOCK)
            block = raw[rows, cols].astype(jnp.float32)
            scale = (jnp.max(jnp.abs(block), axis=1, keepdims=True) + EPSILON).astype(jnp.bfloat16)
            scale = scale.astype(jnp.float32)
            coded = (block / scale).astype(jnp.bfloat16).astype(jnp.float32)
            taken = jnp.where(first, block, coded * scale)
            hidden[rows, cols] = taken
            squares += taken * taken
            scaled[rows, cols] = (taken * gain[0:1, cols]).astype(jnp.bfloat16)
        square_sum[rows, :] += squares

    def inverse_rms(rows):
        mean = jnp.sum(square_sum[rows, :], axis=1, keepdims=True) * (1.0 / MODEL)
        return lax.rsqrt(mean + EPSILON)

    def filled(value):
        return jnp.broadcast_to(value * MARGIN, (SUM_ROWS // 2, HEAD_DIM))

    def longest_square(rows):
        return jnp.max(jnp.sum(rows * rows, axis=1, keepdims=True), axis=0, keepdims=True)

    def store_kv(i, sums, inverse):
        for h in range(KEY_VALUE_HEADS):
            keys = sums[:, h * HEAD_DIM:(h + 1) * HEAD_DIM] * inverse
            kv_out[h, i, 0:HALF, :] = keys.astype(jnp.bfloat16)
            first_col = (KEY_VALUE_HEADS + h) * HEAD_DIM
            values = sums[:, first_col:first_col + HEAD_DIM] * inverse
            kv_out[h, i, HALF:2 * HALF, :] = values.T.astype(jnp.bfloat16)
            largest = jnp.max(jnp.max(jnp.abs(values), axis=0, keepdims=True), axis=1, keepdims=True)
            bounds = jnp.concatenate([filled(longest_square(keys)), filled(largest)], axis=0)
            kv_out[h, i, 2 * HALF:, :] = bounds.astype(jnp.bfloat16)

    def store_q(h, i, sums, q_scale):
        most = jnp.zeros((1, 1), jnp.float32)
        for g in range(GROUP):
            queries = sums[:, g * HEAD_DIM:(g + 1) * HEAD_DIM] * q_scale
            q_out[h, i, g * HALF:(g + 1) * HALF, :] = queries.astype(jnp.bfloat16)
            most = jnp.maximum(most, longest_square(queries))
        q_out[h, i, GROUP * HALF:, :] = jnp.concatenate([filled(most)] * 2, axis=0).astype(jnp.bfloat16)

    def kv_copy(part, i, d):
        return pltpu.make_async_remote_copy(
            kv_out.at[(a + d) % SIDE, part], kv_all.at[b, a, part], kv_send.at[i, d - 1], kv_recv.at[i, d - 1],
            device_id=at((a + d) % SIDE, b), device_id_type=MESH,
        )

    def source(p):
        return (a + SIDE - p) % SIDE

    def row_copy(part, i, p, way):
        block = kv_out.at[a, part] if p == 0 else kv_all.at[b, source(p), part]
        return pltpu.make_async_remote_copy(
            block, kv_all.at[b, source(p), part], row_send.at[i, p, way], row_recv.at[i, p, way],
            device_id=at(a, (b + (1, 3, 2)[way]) % SIDE), device_id_type=MESH,
        )

    def on_copy(part, i, p):
        way = p % 2
        block = kv_all.at[(b + (3, 1)[way]) % SIDE, source(p), part]
        return pltpu.make_async_remote_copy(
            block, block, on_send.at[i, p], on_recv.at[i, p],
            device_id=at(a, (b + (1, 3)[way]) % SIDE), device_id_type=MESH,
        )

    def q_copy(part, i, d):
        return pltpu.make_async_remote_copy(
            q_out.at[(a + d) % SIDE, part], q_all.at[SIDE - d, part], q_send.at[i, d - 1], q_recv.at[i, d - 1],
            device_id=at((a + d) % SIDE, b), device_id_type=MESH,
        )

    def own_kv(part, i):
        return pltpu.make_async_copy(kv_out.at[a, part], kv_all.at[b, a, part], own_sem.at[0, i])

    def own_q(part, i):
        return pltpu.make_async_copy(q_out.at[a, part], q_all.at[0, part], own_sem.at[1, i])

    def hidden_copy(i):
        rows = pl.ds(i * HALF, HALF)
        return pltpu.make_async_copy(hidden.at[rows, :], hidden_out.at[rows, :], hidden_sem.at[i])

    def send_kv(part, i, ways):
        for d in (2, 1, 3):
            kv_copy(part, i, d).start()
        for way in ways:
            row_copy(part, i, 0, way).start()
        own_kv(part, i).start()

    def spread(part, i, ways):
        for p in (1, 3, 2):
            kv_copy(part, i, p).wait_recv()
            for way in ways:
                row_copy(part, i, p, way).start()

    def pass_on(part, i):
        for p in (0, 1, 3, 2):
            row_copy(part, i, p, p % 2).wait_recv()
            on_copy(part, i, p).start()

    def settle(part, i, ways):
        own_kv(part, i).wait()
        own_q(part, i).wait()
        for d in range(1, SIDE):
            q_copy(part, i, d).wait()
            kv_copy(part, i, d).wait_send()
        for p in range(SIDE):
            if len(ways) == 3:
                for way in ways:
                    row_copy(part, i, p, way).wait()
            else:
                row_copy(part, i, p, 1 - p % 2).wait_recv()
                for way in ways:
                    row_copy(part, i, p, way).wait_send()
                on_copy(part, i, p).wait()

    square_sum[...] = jnp.zeros_like(square_sum)
    waits = jnp.logical_and(section % 2 == 0, section > 0)

    @pl.when(waits)
    def _():
        def add_kv(i, k):
            part = pl.ds(pl.multiple_of(k * CHUNK, CHUNK), CHUNK)
            kv_sum[...] += dotf(scaled[pl.ds(i * HALF, HALF), part], kv_w[part, :])

        def add_q(i, k):
            part = pl.ds(pl.multiple_of(k * CHUNK, CHUNK), CHUNK)
            for h in range(KEY_VALUE_HEADS):
                q_sum[h] += dotf(scaled[pl.ds(i * HALF, HALF), part], q_w[h, part, :])

        def take_and_add_kv(i, k, carry):
            take_chunk(i, k)
            add_kv(i, k)
            return carry

        def q_only(i, k, carry):
            add_q(i, k)
            return carry

        def chunk(i, k, carry):
            take_chunk(i, k)
            add_kv(i, k)
            add_q(i, k)
            return carry

        kv_weight_copy.wait()
        for i in range(2):
            part, rows = pl.ds(i, 1), pl.ds(i * HALF, HALF)
            kv_sum[...] = jnp.zeros_like(kv_sum)
            q_sum[...] = jnp.zeros_like(q_sum)
            if i == 0:
                lax.fori_loop(0, N_CHUNK, functools.partial(take_and_add_kv, i), 0)
            else:
                lax.fori_loop(0, N_CHUNK - 1, functools.partial(chunk, i), 0)
                take_and_add_kv(i, N_CHUNK - 1, 0)
            inverse = inverse_rms(rows)
            store_kv(i, kv_sum[...], inverse)
            send_kv(part, i, (RELAYED, DIRECT)[i])
            hidden_copy(i).start()
            if i == 0:
                for d in ORDER:
                    q_weight_copy(d).wait()
                lax.fori_loop(0, N_CHUNK, functools.partial(q_only, i), 0)
            else:
                add_q(i, N_CHUNK - 1)
            q_scale = inverse * Q_SCALE
            for d in ORDER:
                h = (a + d) % SIDE
                store_q(h, i, q_sum[h], q_scale)
                if d:
                    q_copy(part, i, d).start()
                else:
                    own_q(part, i).start()
            if i == 0:
                spread(part, i, RELAYED)
        pass_on(pl.ds(0, 1), 0)
        spread(pl.ds(1, 1), 1, DIRECT)
        settle(pl.ds(0, 1), 0, RELAYED)
        settle(pl.ds(1, 1), 1, DIRECT)

    @pl.when(jnp.logical_not(waits))
    def _():
        for i in range(2):
            for k in range(N_CHUNK):
                take_chunk(i, k)
        kv_weight_copy.wait()
        inverse = inverse_rms(pl.ds(0, ROWS))
        sums = dotf(scaled[...], kv_w[...])
        for i in range(2):
            rows = slice(i * HALF, (i + 1) * HALF)
            store_kv(i, sums[rows, :], inverse[rows, :])
        send_kv(everything, 0, RELAYED)
        for i in range(2):
            hidden_copy(i).start()
        q_scale = inverse * Q_SCALE
        for d in ORDER:
            h = (a + d) % SIDE
            q_weight_copy(d).wait()
            group = dotf(scaled[...], q_w[h])
            for i in range(2):
                rows = slice(i * HALF, (i + 1) * HALF)
                store_q(h, i, group[rows, :], q_scale[rows, :])
            if d:
                q_copy(everything, 0, d).start()
            else:
                own_q(everything, 0).start()
        spread(everything, 0, RELAYED)
        pass_on(everything, 0)
        settle(everything, 0, RELAYED)

    for i in range(2):
        hidden_copy(i).wait()

    @pl.when(section < 7)
    def _():
        for i in range(2):
            for k in range(N_CHUNK):
                hand_off(i, k).wait_send()


def exchange(embedded, finished, gain, q_weight, kv_weight):
    hbm = pl.BlockSpec(memory_space=pltpu.HBM)
    vmem = pltpu.VMEM
    dma = pltpu.SemaphoreType.DMA
    return pl.pallas_call(
        exchange_kernel,
        out_shape=(
            jax.ShapeDtypeStruct((SIDE, 2, Q_PART, HEAD_DIM), jnp.bfloat16),
            jax.ShapeDtypeStruct((SIDE, SIDE, 2, KV_PART, HEAD_DIM), jnp.bfloat16),
            jax.ShapeDtypeStruct((ROWS, MODEL), jnp.float32),
        ),
        in_specs=[hbm, hbm, pl.BlockSpec(memory_space=vmem), hbm, hbm],
        out_specs=(hbm, hbm, hbm),
        scratch_shapes=[
            vmem((ROWS, MODEL), jnp.bfloat16),
            vmem((ROWS, MODEL), jnp.float32),
            vmem((ROWS, MODEL), jnp.bfloat16),
            vmem((SIDE, MODEL, HEAD_COLS), jnp.bfloat16),
            vmem((MODEL, 2 * KEY_VALUE_HEADS * HEAD_DIM), jnp.bfloat16),
            vmem((SIDE, HALF, HEAD_COLS), jnp.float32),
            vmem((HALF, 2 * KEY_VALUE_HEADS * HEAD_DIM), jnp.float32),
            vmem((ROWS, QBLOCK), jnp.float32),
            vmem((SIDE, 2, Q_PART, HEAD_DIM), jnp.bfloat16),
            vmem((SIDE, 2, KV_PART, HEAD_DIM), jnp.bfloat16),
            dma((2, N_CHUNK)), dma((2, N_CHUNK)), dma((SIDE + 1,)), dma((2,)), dma((2, 2)),
            dma((2, 3)), dma((2, 3)), dma((2, SIDE, 3)), dma((2, SIDE, 3)),
            dma((2, SIDE)), dma((2, SIDE)), dma((2, 3)), dma((2, 3)),
        ],
        compiler_params=pltpu.CompilerParams(
            collective_id=0, has_side_effects=True, vmem_limit_bytes=60 << 20
        ),
        cost_estimate=pl.CostEstimate(
            flops=2 * ROWS * MODEL * 3584, bytes_accessed=24 << 20, transcendentals=0
        ),
    )(embedded, finished, gain, q_weight, kv_weight)


def attend_kernel(steps, order, q_all, kv, *refs):
    outs = refs[:len(steps)]
    total, peak, slot_of = refs[len(steps):]
    _, _, a, b, stride_a, stride_b = placement()
    for b_of in range(SIDE):
        for a_of in range(SIDE):
            slot_of[order[a_of * stride_a + b_of * stride_b]] = b_of * SIDE + a_of

    ones = jnp.ones((SUM_ROWS, HEAD_DIM), jnp.bfloat16)
    kv_bounds = jnp.max(kv[:, :, 2 * HALF:, :].astype(jnp.float32), axis=(0, 1))
    q_bounds = jnp.max(q_all[:, :, GROUP * HALF:, :].astype(jnp.float32), axis=(0, 1))
    small = jnp.logical_and(
        jnp.max(kv_bounds[0:SUM_ROWS // 2, :] * q_bounds[0:SUM_ROWS // 2, :]) <= SCORE_LIMIT * SCORE_LIMIT,
        jnp.max(kv_bounds[SUM_ROWS // 2:, :]) <= VALUE_LIMIT,
    )

    def steps_at(i):
        e = steps[0]
        for j in range(1, len(steps)):
            e = jnp.where(i == j, steps[j], e)
        return e

    def query_rows(i):
        return jnp.concatenate([q_all[steps_at(i), half, 0:GROUP * HALF, :] for half in range(2)], axis=0)

    def key_rows(slots):
        return jnp.concatenate(
            [kv[slot, half, 0:HALF, :] for slot in slots for half in range(2)], axis=0
        )

    def value_cols(slots):
        parts = [
            jnp.concatenate([kv[slot, half, HALF:2 * HALF, :], ones], axis=0)
            for slot in slots for half in range(2)
        ]
        return jnp.concatenate(parts, axis=1)

    def causal():
        key = lax.broadcasted_iota(jnp.int32, (ROWS, LANES), 0)
        lane = lax.broadcasted_iota(jnp.int32, (ROWS, LANES), 1)
        return key <= lane % HALF + jnp.where(lane >= LANES // 2, HALF, 0)

    def span(i, carry):
        e = steps_at(i)
        rank = order[((a + e) % SIDE) * stride_a + b * stride_b]

        @pl.when(small)
        def _():
            total[...] = jnp.zeros_like(total)

            def four(c, carry):
                slots = [slot_of[4 * c + j] for j in range(4)]
                weights = jnp.exp2(dotf(key_rows(slots), query_rows(i), NT)).astype(jnp.bfloat16)
                total[...] += dotf(value_cols(slots), weights)
                return carry

            lax.fori_loop(0, rank // 4, four, 0)
            for rest in range(4):

                @pl.when(rank % 4 == rest)
                def _():
                    slots = [slot_of[rank - rest + j] for j in range(rest + 1)]
                    weights = jnp.exp2(dotf(key_rows(slots), query_rows(i), NT))
                    last = jnp.where(causal(), weights[rest * ROWS:, :], 0.0)
                    if rest:
                        last = jnp.concatenate([weights[:rest * ROWS, :], last], axis=0)
                    total[...] += dotf(value_cols(slots), last.astype(jnp.bfloat16))

        @pl.when(jnp.logical_not(small))
        def _():
            total[...] = jnp.zeros_like(total)
            peak[...] = jnp.full_like(peak, MASK_FILLER)

            def one(t, carry):
                slots = [slot_of[t]]
                scores = dotf(key_rows(slots), query_rows(i), NT)
                visible = jnp.logical_or(causal(), t < rank)
                scores = jnp.where(visible, scores, MASK_FILLER)
                before = peak[0:1, :]
                now = jnp.maximum(before, jnp.max(scores, axis=0, keepdims=True))
                weights = jnp.where(visible, jnp.exp2(scores - now), 0.0)
                total[...] = total[...] * jnp.exp2(before - now) + dotf(
                    value_cols(slots), weights.astype(jnp.bfloat16)
                )
                peak[0:1, :] = now
                return carry

            lax.fori_loop(0, rank + 1, one, 0)

        for j in range(len(steps)):

            @pl.when(i == j)
            def _():
                for half in range(2):
                    for g in range(GROUP):
                        first = (half * GROUP + g) * HALF
                        lanes = slice(first, first + HALF)
                        share = total[0:HEAD_DIM, lanes] / total[HEAD_DIM:HEAD_DIM + 1, lanes]
                        rows, cols = slice(half * HALF, (half + 1) * HALF), slice(g * HEAD_DIM, (g + 1) * HEAD_DIM)
                        outs[j][rows, cols] = share.T.astype(jnp.bfloat16)

        return carry

    lax.fori_loop(0, len(steps), span, 0)


def attend(order, q_all, kv_all, steps):
    vmem = pltpu.VMEM
    out = jax.ShapeDtypeStruct((ROWS, HEAD_COLS), jnp.bfloat16)
    n = len(steps)
    return pl.pallas_call(
        functools.partial(attend_kernel, steps),
        out_shape=(out,) * n,
        in_specs=[pl.BlockSpec(memory_space=pltpu.SMEM)] + [pl.BlockSpec(memory_space=vmem)] * 2,
        out_specs=(pl.BlockSpec(memory_space=vmem),) * n,
        scratch_shapes=[
            vmem((HEAD_DIM + SUM_ROWS, LANES), jnp.float32),
            vmem((8, LANES), jnp.float32),
            pltpu.SMEM((SIDE * SIDE,), jnp.int32),
        ],
        compiler_params=pltpu.CompilerParams(vmem_limit_bytes=24 << 20),
        cost_estimate=pl.CostEstimate(
            flops=n * 4 * LANES * HEAD_DIM * 2304, bytes_accessed=3 << 20, transcendentals=n * LANES * 2304
        ),
    )(order, q_all, kv_all.reshape(SIDE * SIDE, 2, KV_PART, HEAD_DIM))


def finish_kernel(p0, p1, p2, p3, hidden, gain, out):
    _, _, a, _, _, _ = placement()
    pieces = [p[...].astype(jnp.float32) for p in (p0, p1, p2, p3)]
    squares = sum(jnp.sum(p * p, axis=1, keepdims=True) for p in pieces)
    inverse = lax.rsqrt(squares * (1.0 / MODEL) + EPSILON)
    for d, piece in enumerate(pieces):
        first = pl.multiple_of(((a + SIDE - d) % SIDE) * HEAD_COLS, HEAD_COLS)
        cols = pl.ds(first, HEAD_COLS)
        rows = hidden[:, cols] + gain[0:1, cols] * (piece * inverse)
        out[:, cols] = rows.astype(jnp.bfloat16)


def finish(pieces, hidden, gain):
    tile = 128
    piece = pl.BlockSpec((tile, HEAD_COLS), lambda i: (i, 0))
    whole = pl.BlockSpec((tile, MODEL), lambda i: (i, 0))
    return pl.pallas_call(
        finish_kernel,
        grid=(ROWS // tile,),
        out_shape=jax.ShapeDtypeStruct((ROWS, MODEL), jnp.bfloat16),
        in_specs=[piece] * 4 + [whole, pl.BlockSpec((1, MODEL), lambda i: (0, 0))],
        out_specs=whole,
        compiler_params=pltpu.CompilerParams(vmem_limit_bytes=16 << 20),
    )(*pieces, hidden, gain)


def send_along(x, d):
    pairs = []
    for section in range(8):
        for ctx in range(16):
            if section % 2:
                to = (ctx + d * SIDE) % 16
            else:
                to = ctx // SIDE * SIDE + (ctx + d) % SIDE
            pairs.append((section * 16 + ctx, section * 16 + to))
    return lax.ppermute(x, ("section", "ctx"), pairs)


def per_device(embedded, finished, norm_gain, q_weight, kv_weight, out_gain, span_order):
    q_all, kv_all, hidden = exchange(
        embedded, finished[0], norm_gain, q_weight[0], kv_weight[0]
    )
    far, near, back = attend(span_order, q_all, kv_all, (2, 1, 3))
    far, near, back = send_along(far, 2), send_along(near, 1), send_along(back, 3)
    (own,) = attend(span_order, q_all, kv_all, (0,))
    return finish((own, near, far, back), hidden, out_gain)[None]


def solution(mesh):
    placed = (
        P("ctx", None),
        P("section", "ctx", None),
        P("section", None),
        P("section", None, None),
        P("section", None, None),
        P("section", None),
        P(),
    )
    return jax.shard_map(
        per_device, mesh=mesh, in_specs=placed, out_specs=P("section", "ctx", None), check_vma=False
    )
```

```python
import functools
import math

import jax
import jax.numpy as jnp
from jax import lax
from jax.experimental import pallas as pl
from jax.experimental.pallas import tpu as pltpu
from jax.sharding import PartitionSpec as P

MESH = pl.DeviceIdType.MESH
QUERY_HEADS = 20
KEY_VALUE_HEADS = 4
GROUP = QUERY_HEADS // KEY_VALUE_HEADS
HEAD_DIM = 128
QBLOCK = 128
EPSILON = 1e-06
MASK_FILLER = -1e30
SIDE = 4
ROWS = 256
HALF = ROWS // 2
MODEL = 2560
HEAD_COLS = GROUP * HEAD_DIM
LANES = GROUP * ROWS
CHUNK = 512
N_CHUNK = MODEL // CHUNK
SUM_ROWS = 16
KV_PART = 2 * HALF + SUM_ROWS
Q_PART = GROUP * HALF + SUM_ROWS
ORDER = (2, 1, 3, 0)
RELAYED, DIRECT = (0, 1), (2, 0, 1)
MARGIN = 1.02
Q_SCALE = HEAD_DIM ** -0.5 * math.log2(math.e)
SCORE_LIMIT = 48.0
VALUE_LIMIT = 1e15

NT = (((1,), (1,)), ((), ()))
NN = (((1,), (0,)), ((), ()))


def dotf(left, right, dims=NN):
    return lax.dot_general(left, right, dims, preferred_element_type=jnp.float32)


def placement():
    section, ctx = lax.axis_index("section"), lax.axis_index("ctx")
    core = section % 2
    stride_a, stride_b = 1 + 3 * core, 4 - 3 * core
    x, y = ctx // SIDE, ctx % SIDE
    a = x * core + y * (1 - core)
    b = y * core + x * (1 - core)
    return section, ctx, a, b, stride_a, stride_b


def exchange_kernel(
    embedded, finished, gain, q_weight, kv_weight,
    q_all, kv_all, hidden_out,
    raw, hidden, scaled, q_w, kv_w, q_sum, kv_sum, square_sum, q_out, kv_out,
    raw_send, raw_recv, w_sem, hidden_sem, own_sem,
    kv_send, kv_recv, row_send, row_recv, on_send, on_recv, q_send, q_recv,
):
    section, ctx, a, b, stride_a, stride_b = placement()
    everything = pl.ds(0, 2)

    def at(a_to, b_to):
        return (section, a_to * stride_a + b_to * stride_b)

    def area(i, k):
        return (
            pl.ds(i * HALF, HALF),
            pl.ds(pl.multiple_of(k * CHUNK, CHUNK), CHUNK),
        )

    def own_chunk(i, k):
        return pltpu.make_async_copy(embedded.at[area(i, k)], raw.at[area(i, k)], raw_recv.at[i, k])

    def hand_off(i, k):
        return pltpu.make_async_remote_copy(
            finished.at[area(i, k)], raw.at[area(i, k)], raw_send.at[i, k], raw_recv.at[i, k],
            device_id=((section + 1) % 8, ctx), device_id_type=MESH,
        )

    kv_weight_copy = pltpu.make_async_copy(kv_weight, kv_w, w_sem.at[SIDE])

    def q_weight_copy(d):
        h = (a + d) % SIDE
        cols = pl.ds(pl.multiple_of(h * HEAD_COLS, HEAD_COLS), HEAD_COLS)
        return pltpu.make_async_copy(q_weight.at[:, cols], q_w.at[h], w_sem.at[d])

    @pl.when(section == 0)
    def _():
        for i in range(2):
            for k in range(N_CHUNK):
                own_chunk(i, k).start()

    barrier = pltpu.get_barrier_semaphore()

    @pl.when(section > 0)
    def _():
        pl.semaphore_signal(barrier, inc=1, device_id=(section - 1, ctx), device_id_type=MESH)

    @pl.when(section < 7)
    def _():
        pl.semaphore_signal(barrier, inc=1, device_id=(section + 1, ctx), device_id_type=MESH)

    for d in range(1, SIDE):
        for peer in (at((a + d) % SIDE, b), at(a, (b + d) % SIDE)):
            pl.semaphore_signal(barrier, inc=1, device_id=peer, device_id_type=MESH)

    kv_weight_copy.start()
    for d in ORDER:
        q_weight_copy(d).start()

    @pl.when(jnp.logical_and(section > 0, section < 7))
    def _():
        pl.semaphore_wait(barrier, 8)

    @pl.when(jnp.logical_or(section == 0, section == 7))
    def _():
        pl.semaphore_wait(barrier, 7)

    @pl.when(section < 7)
    def _():
        for i in range(2):
            for k in range(N_CHUNK):
                hand_off(i, k).start()

    first = section == 0

    def take_chunk(i, k):
        @pl.when(section == 0)
        def _():
            own_chunk(i, k).wait()

        @pl.when(section > 0)
        def _():
            hand_off(i, k).wait_recv()

        rows = pl.ds(i * HALF, HALF)
        squares = jnp.zeros((HALF, QBLOCK), jnp.float32)
        for j in range(CHUNK // QBLOCK):
            cols = pl.ds(pl.multiple_of(k * CHUNK + j * QBLOCK, QBLOCK), QBLOCK)
            block = raw[rows, cols].astype(jnp.float32)
            scale = (jnp.max(jnp.abs(block), axis=1, keepdims=True) + EPSILON).astype(jnp.bfloat16)
            scale = scale.astype(jnp.float32)
            coded = (block / scale).astype(jnp.bfloat16).astype(jnp.float32)
            taken = jnp.where(first, block, coded * scale)
            hidden[rows, cols] = taken
            squares += taken * taken
            scaled[rows, cols] = (taken * gain[0:1, cols]).astype(jnp.bfloat16)
        square_sum[rows, :] += squares

    def inverse_rms(rows):
        mean = jnp.sum(square_sum[rows, :], axis=1, keepdims=True) * (1.0 / MODEL)
        return lax.rsqrt(mean + EPSILON)

    def filled(value):
        return jnp.broadcast_to(value * MARGIN, (SUM_ROWS // 2, HEAD_DIM))

    def longest_square(rows):
        return jnp.max(jnp.sum(rows * rows, axis=1, keepdims=True), axis=0, keepdims=True)

    def store_kv(i, sums, inverse):
        for h in range(KEY_VALUE_HEADS):
            keys = sums[:, h * HEAD_DIM:(h + 1) * HEAD_DIM] * inverse
            kv_out[h, i, 0:HALF, :] = keys.astype(jnp.bfloat16)
            first_col = (KEY_VALUE_HEADS + h) * HEAD_DIM
            values = sums[:, first_col:first_col + HEAD_DIM] * inverse
            kv_out[h, i, HALF:2 * HALF, :] = values.T.astype(jnp.bfloat16)
            largest = jnp.max(jnp.max(jnp.abs(values), axis=0, keepdims=True), axis=1, keepdims=True)
            bounds = jnp.concatenate([filled(longest_square(keys)), filled(largest)], axis=0)
            kv_out[h, i, 2 * HALF:, :] = bounds.astype(jnp.bfloat16)

    def store_q(h, i, sums, q_scale):
        most = jnp.zeros((1, 1), jnp.float32)
        for g in range(GROUP):
            queries = sums[:, g * HEAD_DIM:(g + 1) * HEAD_DIM] * q_scale
            q_out[h, i, g * HALF:(g + 1) * HALF, :] = queries.astype(jnp.bfloat16)
            most = jnp.maximum(most, longest_square(queries))
        q_out[h, i, GROUP * HALF:, :] = jnp.concatenate([filled(most)] * 2, axis=0).astype(jnp.bfloat16)

    def kv_copy(part, i, d):
        return pltpu.make_async_remote_copy(
            kv_out.at[(a + d) % SIDE, part], kv_all.at[b, a, part], kv_send.at[i, d - 1], kv_recv.at[i, d - 1],
            device_id=at((a + d) % SIDE, b), device_id_type=MESH,
        )

    def source(p):
        return (a + SIDE - p) % SIDE

    def row_copy(part, i, p, way):
        block = kv_out.at[a, part] if p == 0 else kv_all.at[b, source(p), part]
        return pltpu.make_async_remote_copy(
            block, kv_all.at[b, source(p), part], row_send.at[i, p, way], row_recv.at[i, p, way],
            device_id=at(a, (b + (1, 3, 2)[way]) % SIDE), device_id_type=MESH,
        )

    def on_copy(part, i, p):
        way = p % 2
        block = kv_all.at[(b + (3, 1)[way]) % SIDE, source(p), part]
        return pltpu.make_async_remote_copy(
            block, block, on_send.at[i, p], on_recv.at[i, p],
            device_id=at(a, (b + (1, 3)[way]) % SIDE), device_id_type=MESH,
        )

    def q_copy(part, i, d):
        return pltpu.make_async_remote_copy(
            q_out.at[(a + d) % SIDE, part], q_all.at[SIDE - d, part], q_send.at[i, d - 1], q_recv.at[i, d - 1],
            device_id=at((a + d) % SIDE, b), device_id_type=MESH,
        )

    def own_kv(part, i):
        return pltpu.make_async_copy(kv_out.at[a, part], kv_all.at[b, a, part], own_sem.at[0, i])

    def own_q(part, i):
        return pltpu.make_async_copy(q_out.at[a, part], q_all.at[0, part], own_sem.at[1, i])

    def hidden_copy(i):
        rows = pl.ds(i * HALF, HALF)
        return pltpu.make_async_copy(hidden.at[rows, :], hidden_out.at[rows, :], hidden_sem.at[i])

    def send_kv(part, i, ways):
        for d in (2, 1, 3):
            kv_copy(part, i, d).start()
        for way in ways:
            row_copy(part, i, 0, way).start()
        own_kv(part, i).start()

    def spread(part, i, ways):
        for p in (1, 3, 2):
            kv_copy(part, i, p).wait_recv()
            for way in ways:
                row_copy(part, i, p, way).start()

    def pass_on(part, i):
        for p in (0, 1, 3, 2):
            row_copy(part, i, p, p % 2).wait_recv()
            on_copy(part, i, p).start()

    def settle(part, i, ways):
        own_kv(part, i).wait()
        own_q(part, i).wait()
        for d in range(1, SIDE):
            kv_copy(part, i, d).wait_send()
            q_copy(part, i, d).wait()
        for p in range(SIDE):
            if len(ways) == 3:
                for way in ways:
                    row_copy(part, i, p, way).wait()
            else:
                row_copy(part, i, p, 1 - p % 2).wait_recv()
                for way in ways:
                    row_copy(part, i, p, way).wait_send()
                on_copy(part, i, p).wait()

    def leave():
        for i in range(2):
            hidden_copy(i).wait()

        @pl.when(section < 7)
        def _():
            for i in range(2):
                for k in range(N_CHUNK):
                    hand_off(i, k).wait_send()

    square_sum[...] = jnp.zeros_like(square_sum)
    waits = jnp.logical_and(section % 2 == 0, section > 0)

    @pl.when(waits)
    def _():
        def add_kv(i, k):
            part = pl.ds(pl.multiple_of(k * CHUNK, CHUNK), CHUNK)
            kv_sum[...] += dotf(scaled[pl.ds(i * HALF, HALF), part], kv_w[part, :])

        def add_q(i, k):
            part = pl.ds(pl.multiple_of(k * CHUNK, CHUNK), CHUNK)
            for h in range(KEY_VALUE_HEADS):
                q_sum[h] += dotf(scaled[pl.ds(i * HALF, HALF), part], q_w[h, part, :])

        def take_and_add_kv(i, k, carry):
            take_chunk(i, k)
            add_kv(i, k)
            return carry

        def q_only(i, k, carry):
            add_q(i, k)
            return carry

        def chunk(i, k, carry):
            take_chunk(i, k)
            add_kv(i, k)
            add_q(i, k)
            return carry

        kv_weight_copy.wait()
        for i in range(2):
            part, rows = pl.ds(i, 1), pl.ds(i * HALF, HALF)
            kv_sum[...] = jnp.zeros_like(kv_sum)
            q_sum[...] = jnp.zeros_like(q_sum)
            if i == 0:
                lax.fori_loop(0, N_CHUNK, functools.partial(take_and_add_kv, i), 0)
            else:
                lax.fori_loop(0, N_CHUNK - 1, functools.partial(chunk, i), 0)
                take_and_add_kv(i, N_CHUNK - 1, 0)
            inverse = inverse_rms(rows)
            store_kv(i, kv_sum[...], inverse)
            send_kv(part, i, (RELAYED, DIRECT)[i])
            hidden_copy(i).start()
            if i == 0:
                for d in ORDER:
                    q_weight_copy(d).wait()
                lax.fori_loop(0, N_CHUNK, functools.partial(q_only, i), 0)
            else:
                add_q(i, N_CHUNK - 1)
            q_scale = inverse * Q_SCALE
            for d in ORDER:
                h = (a + d) % SIDE
                store_q(h, i, q_sum[h], q_scale)
                if d:
                    q_copy(part, i, d).start()
                else:
                    own_q(part, i).start()
            if i == 0:
                spread(part, i, RELAYED)
        pass_on(pl.ds(0, 1), 0)
        spread(pl.ds(1, 1), 1, DIRECT)
        leave()
        settle(pl.ds(0, 1), 0, RELAYED)
        settle(pl.ds(1, 1), 1, DIRECT)

    @pl.when(jnp.logical_not(waits))
    def _():
        for i in range(2):
            for k in range(N_CHUNK):
                take_chunk(i, k)
        kv_weight_copy.wait()
        inverse = inverse_rms(pl.ds(0, ROWS))
        sums = dotf(scaled[...], kv_w[...])
        for i in range(2):
            rows = slice(i * HALF, (i + 1) * HALF)
            store_kv(i, sums[rows, :], inverse[rows, :])
        send_kv(everything, 0, RELAYED)
        for i in range(2):
            hidden_copy(i).start()
        q_scale = inverse * Q_SCALE
        for d in ORDER:
            h = (a + d) % SIDE
            q_weight_copy(d).wait()
            group = dotf(scaled[...], q_w[h])
            for i in range(2):
                rows = slice(i * HALF, (i + 1) * HALF)
                store_q(h, i, group[rows, :], q_scale[rows, :])
            if d:
                q_copy(everything, 0, d).start()
            else:
                own_q(everything, 0).start()
        spread(everything, 0, RELAYED)
        pass_on(everything, 0)
        leave()
        settle(everything, 0, RELAYED)


def exchange(embedded, finished, gain, q_weight, kv_weight):
    hbm = pl.BlockSpec(memory_space=pltpu.HBM)
    vmem = pltpu.VMEM
    dma = pltpu.SemaphoreType.DMA
    return pl.pallas_call(
        exchange_kernel,
        out_shape=(
            jax.ShapeDtypeStruct((SIDE, 2, Q_PART, HEAD_DIM), jnp.bfloat16),
            jax.ShapeDtypeStruct((SIDE, SIDE, 2, KV_PART, HEAD_DIM), jnp.bfloat16),
            jax.ShapeDtypeStruct((ROWS, MODEL), jnp.float32),
        ),
        in_specs=[hbm, hbm, pl.BlockSpec(memory_space=vmem), hbm, hbm],
        out_specs=(hbm, hbm, hbm),
        scratch_shapes=[
            vmem((ROWS, MODEL), jnp.bfloat16),
            vmem((ROWS, MODEL), jnp.float32),
            vmem((ROWS, MODEL), jnp.bfloat16),
            vmem((SIDE, MODEL, HEAD_COLS), jnp.bfloat16),
            vmem((MODEL, 2 * KEY_VALUE_HEADS * HEAD_DIM), jnp.bfloat16),
            vmem((SIDE, HALF, HEAD_COLS), jnp.float32),
            vmem((HALF, 2 * KEY_VALUE_HEADS * HEAD_DIM), jnp.float32),
            vmem((ROWS, QBLOCK), jnp.float32),
            vmem((SIDE, 2, Q_PART, HEAD_DIM), jnp.bfloat16),
            vmem((SIDE, 2, KV_PART, HEAD_DIM), jnp.bfloat16),
            dma((2, N_CHUNK)), dma((2, N_CHUNK)), dma((SIDE + 1,)), dma((2,)), dma((2, 2)),
            dma((2, 3)), dma((2, 3)), dma((2, SIDE, 3)), dma((2, SIDE, 3)),
            dma((2, SIDE)), dma((2, SIDE)), dma((2, 3)), dma((2, 3)),
        ],
        compiler_params=pltpu.CompilerParams(
            collective_id=0, has_side_effects=True, vmem_limit_bytes=44 << 20
        ),
        cost_estimate=pl.CostEstimate(
            flops=2 * ROWS * MODEL * 3584, bytes_accessed=24 << 20, transcendentals=0
        ),
    )(embedded, finished, gain, q_weight, kv_weight)


def attend_kernel(steps, order, q_all, kv, *refs):
    outs = refs[:len(steps)]
    total, peak, slot_of = refs[len(steps):]
    _, _, a, b, stride_a, stride_b = placement()
    for b_of in range(SIDE):
        for a_of in range(SIDE):
            slot_of[order[a_of * stride_a + b_of * stride_b]] = b_of * SIDE + a_of

    ones = jnp.ones((SUM_ROWS, HEAD_DIM), jnp.bfloat16)
    kv_bounds = jnp.max(kv[:, :, 2 * HALF:, :].astype(jnp.float32), axis=(0, 1))
    q_bounds = jnp.max(q_all[:, :, GROUP * HALF:, :].astype(jnp.float32), axis=(0, 1))
    small = jnp.logical_and(
        jnp.max(kv_bounds[0:SUM_ROWS // 2, :] * q_bounds[0:SUM_ROWS // 2, :]) <= SCORE_LIMIT * SCORE_LIMIT,
        jnp.max(kv_bounds[SUM_ROWS // 2:, :]) <= VALUE_LIMIT,
    )

    def steps_at(i):
        e = steps[0]
        for j in range(1, len(steps)):
            e = jnp.where(i == j, steps[j], e)
        return e

    def query_rows(i):
        return jnp.concatenate([q_all[steps_at(i), half, 0:GROUP * HALF, :] for half in range(2)], axis=0)

    def key_rows(slots):
        return jnp.concatenate(
            [kv[slot, half, 0:HALF, :] for slot in slots for half in range(2)], axis=0
        )

    def value_cols(slots):
        parts = [
            jnp.concatenate([kv[slot, half, HALF:2 * HALF, :], ones], axis=0)
            for slot in slots for half in range(2)
        ]
        return jnp.concatenate(parts, axis=1)

    def causal():
        key = lax.broadcasted_iota(jnp.int32, (ROWS, LANES), 0)
        lane = lax.broadcasted_iota(jnp.int32, (ROWS, LANES), 1)
        return key <= lane % HALF + jnp.where(lane >= LANES // 2, HALF, 0)

    def span(i, carry):
        e = steps_at(i)
        rank = order[((a + e) % SIDE) * stride_a + b * stride_b]

        @pl.when(small)
        def _():
            total[...] = jnp.zeros_like(total)

            def blocks(count, c, carry):
                slots = [slot_of[count * c + j] for j in range(count)]
                weights = jnp.exp2(dotf(key_rows(slots), query_rows(i), NT)).astype(jnp.bfloat16)
                total[...] += dotf(value_cols(slots), weights)
                return carry

            lax.fori_loop(0, rank // 8, functools.partial(blocks, 8), 0)

            @pl.when(rank % 8 >= 4)
            def _():
                blocks(4, 2 * (rank // 8), 0)

            for rest in range(4):

                @pl.when(rank % 4 == rest)
                def _():
                    slots = [slot_of[rank - rest + j] for j in range(rest + 1)]
                    weights = jnp.exp2(dotf(key_rows(slots), query_rows(i), NT))
                    last = jnp.where(causal(), weights[rest * ROWS:, :], 0.0)
                    if rest:
                        last = jnp.concatenate([weights[:rest * ROWS, :], last], axis=0)
                    total[...] += dotf(value_cols(slots), last.astype(jnp.bfloat16))

        @pl.when(jnp.logical_not(small))
        def _():
            total[...] = jnp.zeros_like(total)
            peak[...] = jnp.full_like(peak, MASK_FILLER)

            def one(t, carry):
                slots = [slot_of[t]]
                scores = dotf(key_rows(slots), query_rows(i), NT)
                visible = jnp.logical_or(causal(), t < rank)
                scores = jnp.where(visible, scores, MASK_FILLER)
                before = peak[0:1, :]
                now = jnp.maximum(before, jnp.max(scores, axis=0, keepdims=True))
                weights = jnp.where(visible, jnp.exp2(scores - now), 0.0)
                total[...] = total[...] * jnp.exp2(before - now) + dotf(
                    value_cols(slots), weights.astype(jnp.bfloat16)
                )
                peak[0:1, :] = now
                return carry

            lax.fori_loop(0, rank + 1, one, 0)

        for j in range(len(steps)):

            @pl.when(i == j)
            def _():
                for half in range(2):
                    for g in range(GROUP):
                        first = (half * GROUP + g) * HALF
                        lanes = slice(first, first + HALF)
                        share = total[0:HEAD_DIM, lanes] / total[HEAD_DIM:HEAD_DIM + 1, lanes]
                        rows, cols = slice(half * HALF, (half + 1) * HALF), slice(g * HEAD_DIM, (g + 1) * HEAD_DIM)
                        outs[j][rows, cols] = share.T.astype(jnp.bfloat16)

        return carry

    lax.fori_loop(0, len(steps), span, 0)


def attend(order, q_all, kv_all, steps):
    vmem = pltpu.VMEM
    out = jax.ShapeDtypeStruct((ROWS, HEAD_COLS), jnp.bfloat16)
    n = len(steps)
    return pl.pallas_call(
        functools.partial(attend_kernel, steps),
        out_shape=(out,) * n,
        in_specs=[pl.BlockSpec(memory_space=pltpu.SMEM)] + [pl.BlockSpec(memory_space=vmem)] * 2,
        out_specs=(pl.BlockSpec(memory_space=vmem),) * n,
        scratch_shapes=[
            vmem((HEAD_DIM + SUM_ROWS, LANES), jnp.float32),
            vmem((8, LANES), jnp.float32),
            pltpu.SMEM((SIDE * SIDE,), jnp.int32),
        ],
        compiler_params=pltpu.CompilerParams(vmem_limit_bytes=24 << 20),
        cost_estimate=pl.CostEstimate(
            flops=n * 4 * LANES * HEAD_DIM * 2304, bytes_accessed=3 << 20, transcendentals=n * LANES * 2304
        ),
    )(order, q_all, kv_all.reshape(SIDE * SIDE, 2, KV_PART, HEAD_DIM))


def finish_kernel(p0, p1, p2, p3, hidden, gain, out):
    _, _, a, _, _, _ = placement()
    pieces = [p[...].astype(jnp.float32) for p in (p0, p1, p2, p3)]
    squares = sum(jnp.sum(p * p, axis=1, keepdims=True) for p in pieces)
    inverse = lax.rsqrt(squares * (1.0 / MODEL) + EPSILON)
    for d, piece in enumerate(pieces):
        first = pl.multiple_of(((a + SIDE - d) % SIDE) * HEAD_COLS, HEAD_COLS)
        cols = pl.ds(first, HEAD_COLS)
        rows = hidden[:, cols] + gain[0:1, cols] * (piece * inverse)
        out[:, cols] = rows.astype(jnp.bfloat16)


def finish(pieces, hidden, gain):
    tile = 128
    piece = pl.BlockSpec((tile, HEAD_COLS), lambda i: (i, 0))
    whole = pl.BlockSpec((tile, MODEL), lambda i: (i, 0))
    return pl.pallas_call(
        finish_kernel,
        grid=(ROWS // tile,),
        out_shape=jax.ShapeDtypeStruct((ROWS, MODEL), jnp.bfloat16),
        in_specs=[piece] * 4 + [whole, pl.BlockSpec((1, MODEL), lambda i: (0, 0))],
        out_specs=whole,
        compiler_params=pltpu.CompilerParams(vmem_limit_bytes=16 << 20),
    )(*pieces, hidden, gain)


def send_along(x, d):
    pairs = []
    for section in range(8):
        for ctx in range(16):
            if section % 2:
                to = (ctx + d * SIDE) % 16
            else:
                to = ctx // SIDE * SIDE + (ctx + d) % SIDE
            pairs.append((section * 16 + ctx, section * 16 + to))
    return lax.ppermute(x, ("section", "ctx"), pairs)


def per_device(embedded, finished, norm_gain, q_weight, kv_weight, out_gain, span_order):
    q_all, kv_all, hidden = exchange(
        embedded, finished[0], norm_gain, q_weight[0], kv_weight[0]
    )
    far, near, back = attend(span_order, q_all, kv_all, (2, 1, 3))
    far, near, back = send_along(far, 2), send_along(near, 1), send_along(back, 3)
    (own,) = attend(span_order, q_all, kv_all, (0,))
    return finish((own, near, far, back), hidden, out_gain)[None]


def solution(mesh):
    placed = (
        P("ctx", None),
        P("section", "ctx", None),
        P("section", None),
        P("section", None, None),
        P("section", None, None),
        P("section", None),
        P(),
    )
    return jax.shard_map(
        per_device, mesh=mesh, in_specs=placed, out_specs=P("section", "ctx", None), check_vma=False
    )
```

```python
import functools
import math

import jax
import jax.numpy as jnp
from jax import lax
from jax.experimental import pallas as pl
from jax.experimental.pallas import tpu as pltpu
from jax.sharding import PartitionSpec as P

MESH = pl.DeviceIdType.MESH
QUERY_HEADS = 20
KEY_VALUE_HEADS = 4
GROUP = QUERY_HEADS // KEY_VALUE_HEADS
HEAD_DIM = 128
QBLOCK = 128
EPSILON = 1e-06
MASK_FILLER = -1e30
SIDE = 4
ROWS = 256
HALF = ROWS // 2
MODEL = 2560
HEAD_COLS = GROUP * HEAD_DIM
LANES = GROUP * ROWS
CHUNK = 512
N_CHUNK = MODEL // CHUNK
SUM_ROWS = 16
KV_PART = 2 * HALF + SUM_ROWS
Q_PART = GROUP * HALF + SUM_ROWS
ORDER = (2, 1, 3, 0)
RELAYED, DIRECT = (0, 1), (2, 0, 1)
MARGIN = 1.02
Q_SCALE = HEAD_DIM ** -0.5 * math.log2(math.e)
SCORE_LIMIT = 48.0
VALUE_LIMIT = 1e15

NT = (((1,), (1,)), ((), ()))
NN = (((1,), (0,)), ((), ()))


def dotf(left, right, dims=NN):
    return lax.dot_general(left, right, dims, preferred_element_type=jnp.float32)


def placement():
    section, ctx = lax.axis_index("section"), lax.axis_index("ctx")
    core = section % 2
    stride_a, stride_b = 1 + 3 * core, 4 - 3 * core
    x, y = ctx // SIDE, ctx % SIDE
    a = x * core + y * (1 - core)
    b = y * core + x * (1 - core)
    return section, ctx, a, b, stride_a, stride_b


def exchange_kernel(
    embedded, finished, gain_hbm, q_weight, kv_weight,
    q_all, kv_all, hidden_out,
    gain, raw, hidden, scaled, q_w, kv_w, q_sum, kv_sum, square_sum, q_out, kv_out,
    raw_send, raw_recv, w_sem, hidden_sem, own_sem,
    kv_send, kv_recv, row_send, row_recv, on_send, on_recv, q_send, q_recv,
):
    section, ctx, a, b, stride_a, stride_b = placement()
    everything = pl.ds(0, 2)

    def at(a_to, b_to):
        return (section, a_to * stride_a + b_to * stride_b)

    def area(i, k):
        return (
            pl.ds(i * HALF, HALF),
            pl.ds(pl.multiple_of(k * CHUNK, CHUNK), CHUNK),
        )

    def own_chunk(i, k):
        return pltpu.make_async_copy(embedded.at[area(i, k)], raw.at[area(i, k)], raw_recv.at[i, k])

    def hand_off(i, k):
        return pltpu.make_async_remote_copy(
            finished.at[area(i, k)], raw.at[area(i, k)], raw_send.at[i, k], raw_recv.at[i, k],
            device_id=((section + 1) % 8, ctx), device_id_type=MESH,
        )

    kv_weight_copy = pltpu.make_async_copy(kv_weight, kv_w, w_sem.at[SIDE])
    gain_copy = pltpu.make_async_copy(gain_hbm, gain, w_sem.at[SIDE + 1])
    gain_copy.start()

    def q_weight_copy(d):
        h = (a + d) % SIDE
        cols = pl.ds(pl.multiple_of(h * HEAD_COLS, HEAD_COLS), HEAD_COLS)
        return pltpu.make_async_copy(q_weight.at[:, cols], q_w.at[h], w_sem.at[d])

    @pl.when(section == 0)
    def _():
        for i in range(2):
            for k in range(N_CHUNK):
                own_chunk(i, k).start()

    barrier = pltpu.get_barrier_semaphore()

    @pl.when(section > 0)
    def _():
        pl.semaphore_signal(barrier, inc=1, device_id=(section - 1, ctx), device_id_type=MESH)

    @pl.when(section < 7)
    def _():
        pl.semaphore_signal(barrier, inc=1, device_id=(section + 1, ctx), device_id_type=MESH)

    for d in range(1, SIDE):
        for peer in (at((a + d) % SIDE, b), at(a, (b + d) % SIDE)):
            pl.semaphore_signal(barrier, inc=1, device_id=peer, device_id_type=MESH)

    kv_weight_copy.start()
    for d in ORDER:
        q_weight_copy(d).start()

    @pl.when(jnp.logical_and(section > 0, section < 7))
    def _():
        pl.semaphore_wait(barrier, 8)

    @pl.when(jnp.logical_or(section == 0, section == 7))
    def _():
        pl.semaphore_wait(barrier, 7)

    @pl.when(section < 7)
    def _():
        for i in range(2):
            for k in range(N_CHUNK):
                hand_off(i, k).start()

    first = section == 0

    def take_chunk(i, k):
        @pl.when(section == 0)
        def _():
            own_chunk(i, k).wait()

        @pl.when(section > 0)
        def _():
            hand_off(i, k).wait_recv()

        rows = pl.ds(i * HALF, HALF)
        squares = jnp.zeros((HALF, QBLOCK), jnp.float32)
        for j in range(CHUNK // QBLOCK):
            cols = pl.ds(pl.multiple_of(k * CHUNK + j * QBLOCK, QBLOCK), QBLOCK)
            block = raw[rows, cols].astype(jnp.float32)
            scale = (jnp.max(jnp.abs(block), axis=1, keepdims=True) + EPSILON).astype(jnp.bfloat16)
            scale = scale.astype(jnp.float32)
            coded = (block / scale).astype(jnp.bfloat16).astype(jnp.float32)
            taken = jnp.where(first, block, coded * scale)
            hidden[rows, cols] = taken
            squares += taken * taken
            scaled[rows, cols] = (taken * gain[0:1, cols]).astype(jnp.bfloat16)
        square_sum[rows, :] += squares

    def inverse_rms(rows):
        mean = jnp.sum(square_sum[rows, :], axis=1, keepdims=True) * (1.0 / MODEL)
        return lax.rsqrt(mean + EPSILON)

    def filled(value):
        return jnp.broadcast_to(value * MARGIN, (SUM_ROWS // 2, HEAD_DIM))

    def longest_square(rows):
        return jnp.max(jnp.sum(rows * rows, axis=1, keepdims=True), axis=0, keepdims=True)

    def store_kv(i, sums, inverse):
        for h in range(KEY_VALUE_HEADS):
            keys = sums[:, h * HEAD_DIM:(h + 1) * HEAD_DIM] * inverse
            kv_out[h, i, 0:HALF, :] = keys.astype(jnp.bfloat16)
            first_col = (KEY_VALUE_HEADS + h) * HEAD_DIM
            values = sums[:, first_col:first_col + HEAD_DIM] * inverse
            kv_out[h, i, HALF:2 * HALF, :] = values.T.astype(jnp.bfloat16)
            largest = jnp.max(jnp.max(jnp.abs(values), axis=0, keepdims=True), axis=1, keepdims=True)
            bounds = jnp.concatenate([filled(longest_square(keys)), filled(largest)], axis=0)
            kv_out[h, i, 2 * HALF:, :] = bounds.astype(jnp.bfloat16)

    def store_q(h, i, sums, q_scale):
        most = jnp.zeros((1, 1), jnp.float32)
        for g in range(GROUP):
            queries = sums[:, g * HEAD_DIM:(g + 1) * HEAD_DIM] * q_scale
            q_out[h, i, g * HALF:(g + 1) * HALF, :] = queries.astype(jnp.bfloat16)
            most = jnp.maximum(most, longest_square(queries))
        q_out[h, i, GROUP * HALF:, :] = jnp.concatenate([filled(most)] * 2, axis=0).astype(jnp.bfloat16)

    def kv_copy(part, i, d):
        return pltpu.make_async_remote_copy(
            kv_out.at[(a + d) % SIDE, part], kv_all.at[b, a, part], kv_send.at[i, d - 1], kv_recv.at[i, d - 1],
            device_id=at((a + d) % SIDE, b), device_id_type=MESH,
        )

    def source(p):
        return (a + SIDE - p) % SIDE

    def row_copy(part, i, p, way):
        block = kv_out.at[a, part] if p == 0 else kv_all.at[b, source(p), part]
        return pltpu.make_async_remote_copy(
            block, kv_all.at[b, source(p), part], row_send.at[i, p, way], row_recv.at[i, p, way],
            device_id=at(a, (b + (1, 3, 2)[way]) % SIDE), device_id_type=MESH,
        )

    def on_copy(part, i, p):
        way = p % 2
        block = kv_all.at[(b + (3, 1)[way]) % SIDE, source(p), part]
        return pltpu.make_async_remote_copy(
            block, block, on_send.at[i, p], on_recv.at[i, p],
            device_id=at(a, (b + (1, 3)[way]) % SIDE), device_id_type=MESH,
        )

    def q_copy(part, i, d):
        return pltpu.make_async_remote_copy(
            q_out.at[(a + d) % SIDE, part], q_all.at[SIDE - d, part], q_send.at[i, d - 1], q_recv.at[i, d - 1],
            device_id=at((a + d) % SIDE, b), device_id_type=MESH,
        )

    def own_kv(part, i):
        return pltpu.make_async_copy(kv_out.at[a, part], kv_all.at[b, a, part], own_sem.at[0, i])

    def own_q(part, i):
        return pltpu.make_async_copy(q_out.at[a, part], q_all.at[0, part], own_sem.at[1, i])

    def hidden_copy(i):
        rows = pl.ds(i * HALF, HALF)
        return pltpu.make_async_copy(hidden.at[rows, :], hidden_out.at[rows, :], hidden_sem.at[i])

    def send_kv(part, i, ways):
        for d in (2, 1, 3):
            kv_copy(part, i, d).start()
        for way in ways:
            row_copy(part, i, 0, way).start()
        own_kv(part, i).start()

    def spread(part, i, ways):
        for p in (1, 3, 2):
            kv_copy(part, i, p).wait_recv()
            for way in ways:
                row_copy(part, i, p, way).start()

    def pass_on(part, i):
        for p in (0, 1, 3, 2):
            row_copy(part, i, p, p % 2).wait_recv()
            on_copy(part, i, p).start()

    def settle(part, i, ways):
        own_kv(part, i).wait()
        own_q(part, i).wait()
        for d in range(1, SIDE):
            kv_copy(part, i, d).wait_send()
            q_copy(part, i, d).wait()
        for p in range(SIDE):
            if len(ways) == 3:
                for way in ways:
                    row_copy(part, i, p, way).wait()
            else:
                row_copy(part, i, p, 1 - p % 2).wait_recv()
                for way in ways:
                    row_copy(part, i, p, way).wait_send()
                on_copy(part, i, p).wait()

    def leave():
        for i in range(2):
            hidden_copy(i).wait()

        @pl.when(section < 7)
        def _():
            for i in range(2):
                for k in range(N_CHUNK):
                    hand_off(i, k).wait_send()

    square_sum[...] = jnp.zeros_like(square_sum)
    gain_copy.wait()
    waits = jnp.logical_and(section % 2 == 0, section > 0)

    @pl.when(waits)
    def _():
        def add_kv(i, k):
            part = pl.ds(pl.multiple_of(k * CHUNK, CHUNK), CHUNK)
            kv_sum[...] += dotf(scaled[pl.ds(i * HALF, HALF), part], kv_w[part, :])

        def add_q(i, k):
            part = pl.ds(pl.multiple_of(k * CHUNK, CHUNK), CHUNK)
            for h in range(KEY_VALUE_HEADS):
                q_sum[h] += dotf(scaled[pl.ds(i * HALF, HALF), part], q_w[h, part, :])

        def take_and_add_kv(i, k, carry):
            take_chunk(i, k)
            add_kv(i, k)
            return carry

        def q_only(i, k, carry):
            add_q(i, k)
            return carry

        def chunk(i, k, carry):
            take_chunk(i, k)
            add_kv(i, k)
            add_q(i, k)
            return carry

        kv_weight_copy.wait()
        for i in range(2):
            part, rows = pl.ds(i, 1), pl.ds(i * HALF, HALF)
            kv_sum[...] = jnp.zeros_like(kv_sum)
            q_sum[...] = jnp.zeros_like(q_sum)
            if i == 0:
                lax.fori_loop(0, N_CHUNK, functools.partial(take_and_add_kv, i), 0)
            else:
                lax.fori_loop(0, N_CHUNK - 1, functools.partial(chunk, i), 0)
                take_and_add_kv(i, N_CHUNK - 1, 0)
            inverse = inverse_rms(rows)
            store_kv(i, kv_sum[...], inverse)
            send_kv(part, i, (RELAYED, DIRECT)[i])
            hidden_copy(i).start()
            if i == 0:
                for d in ORDER:
                    q_weight_copy(d).wait()
                lax.fori_loop(0, N_CHUNK, functools.partial(q_only, i), 0)
            else:
                add_q(i, N_CHUNK - 1)
            q_scale = inverse * Q_SCALE
            for d in ORDER:
                h = (a + d) % SIDE
                store_q(h, i, q_sum[h], q_scale)
                if d:
                    q_copy(part, i, d).start()
                else:
                    own_q(part, i).start()
            if i == 0:
                spread(part, i, RELAYED)
        pass_on(pl.ds(0, 1), 0)
        spread(pl.ds(1, 1), 1, DIRECT)
        leave()
        settle(pl.ds(0, 1), 0, RELAYED)
        settle(pl.ds(1, 1), 1, DIRECT)

    @pl.when(jnp.logical_not(waits))
    def _():
        for i in range(2):
            for k in range(N_CHUNK):
                take_chunk(i, k)
        kv_weight_copy.wait()
        inverse = inverse_rms(pl.ds(0, ROWS))
        sums = dotf(scaled[...], kv_w[...])
        for i in range(2):
            rows = slice(i * HALF, (i + 1) * HALF)
            store_kv(i, sums[rows, :], inverse[rows, :])
        send_kv(everything, 0, RELAYED)
        for i in range(2):
            hidden_copy(i).start()
        q_scale = inverse * Q_SCALE
        for d in ORDER:
            h = (a + d) % SIDE
            q_weight_copy(d).wait()
            group = dotf(scaled[...], q_w[h])
            for i in range(2):
                rows = slice(i * HALF, (i + 1) * HALF)
                store_q(h, i, group[rows, :], q_scale[rows, :])
            if d:
                q_copy(everything, 0, d).start()
            else:
                own_q(everything, 0).start()
        spread(everything, 0, RELAYED)
        pass_on(everything, 0)
        leave()
        settle(everything, 0, RELAYED)


def exchange(embedded, finished, gain, q_weight, kv_weight):
    hbm = pl.BlockSpec(memory_space=pltpu.HBM)
    vmem = pltpu.VMEM
    dma = pltpu.SemaphoreType.DMA
    return pl.pallas_call(
        exchange_kernel,
        out_shape=(
            jax.ShapeDtypeStruct((SIDE, 2, Q_PART, HEAD_DIM), jnp.bfloat16),
            jax.ShapeDtypeStruct((SIDE, SIDE, 2, KV_PART, HEAD_DIM), jnp.bfloat16),
            jax.ShapeDtypeStruct((ROWS, MODEL), jnp.float32),
        ),
        in_specs=[hbm] * 5,
        out_specs=(hbm, hbm, hbm),
        scratch_shapes=[
            vmem((1, MODEL), jnp.float32),
            vmem((ROWS, MODEL), jnp.bfloat16),
            vmem((ROWS, MODEL), jnp.float32),
            vmem((ROWS, MODEL), jnp.bfloat16),
            vmem((SIDE, MODEL, HEAD_COLS), jnp.bfloat16),
            vmem((MODEL, 2 * KEY_VALUE_HEADS * HEAD_DIM), jnp.bfloat16),
            vmem((SIDE, HALF, HEAD_COLS), jnp.float32),
            vmem((HALF, 2 * KEY_VALUE_HEADS * HEAD_DIM), jnp.float32),
            vmem((ROWS, QBLOCK), jnp.float32),
            vmem((SIDE, 2, Q_PART, HEAD_DIM), jnp.bfloat16),
            vmem((SIDE, 2, KV_PART, HEAD_DIM), jnp.bfloat16),
            dma((2, N_CHUNK)), dma((2, N_CHUNK)), dma((SIDE + 2,)), dma((2,)), dma((2, 2)),
            dma((2, 3)), dma((2, 3)), dma((2, SIDE, 3)), dma((2, SIDE, 3)),
            dma((2, SIDE)), dma((2, SIDE)), dma((2, 3)), dma((2, 3)),
        ],
        compiler_params=pltpu.CompilerParams(
            collective_id=0, has_side_effects=True, vmem_limit_bytes=44 << 20
        ),
        cost_estimate=pl.CostEstimate(
            flops=2 * ROWS * MODEL * 3584, bytes_accessed=24 << 20, transcendentals=0
        ),
    )(*[pltpu.with_memory_space_constraint(x, pltpu.HBM) for x in (embedded, finished, gain)], q_weight, kv_weight)


def attend_kernel(steps, order, q_all, kv, *refs):
    outs = refs[:len(steps)]
    total, peak, slot_of = refs[len(steps):]
    _, _, a, b, stride_a, stride_b = placement()
    for b_of in range(SIDE):
        for a_of in range(SIDE):
            slot_of[order[a_of * stride_a + b_of * stride_b]] = b_of * SIDE + a_of

    ones = jnp.ones((SUM_ROWS, HEAD_DIM), jnp.bfloat16)
    kv_bounds = jnp.max(kv[:, :, 2 * HALF:, :].astype(jnp.float32), axis=(0, 1))
    q_bounds = jnp.max(q_all[:, :, GROUP * HALF:, :].astype(jnp.float32), axis=(0, 1))
    small = jnp.logical_and(
        jnp.max(kv_bounds[0:SUM_ROWS // 2, :] * q_bounds[0:SUM_ROWS // 2, :]) <= SCORE_LIMIT * SCORE_LIMIT,
        jnp.max(kv_bounds[SUM_ROWS // 2:, :]) <= VALUE_LIMIT,
    )

    def steps_at(i):
        e = steps[0]
        for j in range(1, len(steps)):
            e = jnp.where(i == j, steps[j], e)
        return e

    def query_rows(i):
        return jnp.concatenate([q_all[steps_at(i), half, 0:GROUP * HALF, :] for half in range(2)], axis=0)

    def key_rows(slots):
        return jnp.concatenate(
            [kv[slot, half, 0:HALF, :] for slot in slots for half in range(2)], axis=0
        )

    def value_cols(slots):
        parts = [
            jnp.concatenate([kv[slot, half, HALF:2 * HALF, :], ones], axis=0)
            for slot in slots for half in range(2)
        ]
        return jnp.concatenate(parts, axis=1)

    def causal():
        key = lax.broadcasted_iota(jnp.int32, (ROWS, LANES), 0)
        lane = lax.broadcasted_iota(jnp.int32, (ROWS, LANES), 1)
        return key <= lane % HALF + jnp.where(lane >= LANES // 2, HALF, 0)

    def span(i, carry):
        e = steps_at(i)
        rank = order[((a + e) % SIDE) * stride_a + b * stride_b]

        @pl.when(small)
        def _():
            total[...] = jnp.zeros_like(total)

            def blocks(count, c, carry):
                slots = [slot_of[count * c + j] for j in range(count)]
                weights = jnp.exp2(dotf(key_rows(slots), query_rows(i), NT)).astype(jnp.bfloat16)
                total[...] += dotf(value_cols(slots), weights)
                return carry

            lax.fori_loop(0, rank // 8, functools.partial(blocks, 8), 0)

            @pl.when(rank % 8 >= 4)
            def _():
                blocks(4, 2 * (rank // 8), 0)

            for rest in range(4):

                @pl.when(rank % 4 == rest)
                def _():
                    slots = [slot_of[rank - rest + j] for j in range(rest + 1)]
                    weights = jnp.exp2(dotf(key_rows(slots), query_rows(i), NT))
                    last = jnp.where(causal(), weights[rest * ROWS:, :], 0.0)
                    if rest:
                        last = jnp.concatenate([weights[:rest * ROWS, :], last], axis=0)
                    total[...] += dotf(value_cols(slots), last.astype(jnp.bfloat16))

        @pl.when(jnp.logical_not(small))
        def _():
            total[...] = jnp.zeros_like(total)
            peak[...] = jnp.full_like(peak, MASK_FILLER)

            def one(t, carry):
                slots = [slot_of[t]]
                scores = dotf(key_rows(slots), query_rows(i), NT)
                visible = jnp.logical_or(causal(), t < rank)
                scores = jnp.where(visible, scores, MASK_FILLER)
                before = peak[0:1, :]
                now = jnp.maximum(before, jnp.max(scores, axis=0, keepdims=True))
                weights = jnp.where(visible, jnp.exp2(scores - now), 0.0)
                total[...] = total[...] * jnp.exp2(before - now) + dotf(
                    value_cols(slots), weights.astype(jnp.bfloat16)
                )
                peak[0:1, :] = now
                return carry

            lax.fori_loop(0, rank + 1, one, 0)

        for j in range(len(steps)):

            @pl.when(i == j)
            def _():
                for half in range(2):
                    for g in range(GROUP):
                        first = (half * GROUP + g) * HALF
                        lanes = slice(first, first + HALF)
                        share = total[0:HEAD_DIM, lanes] / total[HEAD_DIM:HEAD_DIM + 1, lanes]
                        rows, cols = slice(half * HALF, (half + 1) * HALF), slice(g * HEAD_DIM, (g + 1) * HEAD_DIM)
                        outs[j][rows, cols] = share.T.astype(jnp.bfloat16)

        return carry

    lax.fori_loop(0, len(steps), span, 0)


def attend(order, q_all, kv_all, steps):
    vmem = pltpu.VMEM
    out = jax.ShapeDtypeStruct((ROWS, HEAD_COLS), jnp.bfloat16)
    n = len(steps)
    return pl.pallas_call(
        functools.partial(attend_kernel, steps),
        out_shape=(out,) * n,
        in_specs=[pl.BlockSpec(memory_space=pltpu.SMEM)] + [pl.BlockSpec(memory_space=vmem)] * 2,
        out_specs=(pl.BlockSpec(memory_space=vmem),) * n,
        scratch_shapes=[
            vmem((HEAD_DIM + SUM_ROWS, LANES), jnp.float32),
            vmem((8, LANES), jnp.float32),
            pltpu.SMEM((SIDE * SIDE,), jnp.int32),
        ],
        compiler_params=pltpu.CompilerParams(vmem_limit_bytes=24 << 20),
        cost_estimate=pl.CostEstimate(
            flops=n * 4 * LANES * HEAD_DIM * 2304, bytes_accessed=3 << 20, transcendentals=n * LANES * 2304
        ),
    )(order, q_all, kv_all.reshape(SIDE * SIDE, 2, KV_PART, HEAD_DIM))


def finish_kernel(p0, p1, p2, p3, hidden, gain, out):
    _, _, a, _, _, _ = placement()
    pieces = [p[...].astype(jnp.float32) for p in (p0, p1, p2, p3)]
    squares = sum(jnp.sum(p * p, axis=1, keepdims=True) for p in pieces)
    inverse = lax.rsqrt(squares * (1.0 / MODEL) + EPSILON)
    for d, piece in enumerate(pieces):
        first = pl.multiple_of(((a + SIDE - d) % SIDE) * HEAD_COLS, HEAD_COLS)
        cols = pl.ds(first, HEAD_COLS)
        rows = hidden[:, cols] + gain[0:1, cols] * (piece * inverse)
        out[:, cols] = rows.astype(jnp.bfloat16)


def finish(pieces, hidden, gain):
    tile = 128
    piece = pl.BlockSpec((tile, HEAD_COLS), lambda i: (i, 0))
    whole = pl.BlockSpec((tile, MODEL), lambda i: (i, 0))
    return pl.pallas_call(
        finish_kernel,
        grid=(ROWS // tile,),
        out_shape=jax.ShapeDtypeStruct((ROWS, MODEL), jnp.bfloat16),
        in_specs=[piece] * 4 + [whole, pl.BlockSpec((1, MODEL), lambda i: (0, 0))],
        out_specs=whole,
        compiler_params=pltpu.CompilerParams(vmem_limit_bytes=16 << 20),
    )(*pieces, hidden, gain)


def send_along(x, d):
    pairs = []
    for section in range(8):
        for ctx in range(16):
            if section % 2:
                to = (ctx + d * SIDE) % 16
            else:
                to = ctx // SIDE * SIDE + (ctx + d) % SIDE
            pairs.append((section * 16 + ctx, section * 16 + to))
    return lax.ppermute(x, ("section", "ctx"), pairs)


def per_device(embedded, finished, norm_gain, q_weight, kv_weight, out_gain, span_order):
    q_all, kv_all, hidden = exchange(
        embedded, finished[0], norm_gain, q_weight[0], kv_weight[0]
    )
    far, near, back = attend(span_order, q_all, kv_all, (2, 1, 3))
    far, near, back = send_along(far, 2), send_along(near, 1), send_along(back, 3)
    (own,) = attend(span_order, q_all, kv_all, (0,))
    return finish((own, near, far, back), hidden, out_gain)[None]


def solution(mesh):
    placed = (
        P("ctx", None),
        P("section", "ctx", None),
        P("section", None),
        P("section", None, None),
        P("section", None, None),
        P("section", None),
        P(),
    )
    return jax.shard_map(
        per_device, mesh=mesh, in_specs=placed, out_specs=P("section", "ctx", None), check_vma=False
    )
```
